128 devices in a mesh: az: 16 (over x, y_lo, core), ax: 8 (over y_hi, z).
Axes of the slice: x: 4, y: 4 (y_hi: 2, y_lo: 2; y = y_hi * 2 + y_lo), z: 4, core: 2. Of those that a mesh axis runs over, the one named last changes fastest.
Arguments:
- fields: float32 [3, 64, 1024, 512], P(None, 'ax', 'az'), may hold values from -4.5 to 4.5
- conduct: float32 [1024, 512], P('az'), may hold values from 6000 to 24001
- kernel: float32 [128, 1024], P('ax', 'az'), may hold values from -0.1875 to 0.1875
Outputs:
- section: float32 [3, 64, 1024, 512], P(None, 'ax', 'az')
The draws below stay inside these ranges and needn't reach their ends.
All inputs are finite; a program needn't handle non-finite values.
Results may differ from the reference program's by a relative error of at most 0.00035.
Values sent between devices are 32-bit elements; how exact they have to be, the bound alone decides.
A program may use at most 128 MiB of HBM per device.

```python
import math
import jax
import jax.numpy as jnp
from jax import lax

NF = 3
NAZ = 1024
NR = 512
NEAR = 128
AXIAL = 64


def draw_fields(key, part):
    shape = (NF, AXIAL, NAZ, NR)
    rough_key = jax.random.fold_in(key, 11)
    phase_key = jax.random.fold_in(key, 23)
    azimuth = jnp.arange(NAZ, dtype=jnp.float32)[None, None, :, None]
    rough = jax.random.truncated_normal(rough_key, -3.0, 3.0, shape, jnp.float32)
    offset = jax.random.uniform(phase_key, (NF, AXIAL, 1, NR), jnp.float32, 0.0, 2.0 * math.pi)
    smooth = 1.5 * jnp.cos(2.0 * math.pi * azimuth / NAZ + offset)
    return rough + smooth


def draw_conduct(key, part):
    cycles = jnp.arange(NR, dtype=jnp.float32)
    base = 12000.0 / (1.0 + cycles / NR)
    factor = jnp.exp(jax.random.uniform(key, (NAZ, NR), jnp.float32, 0.0, math.log(2.0)))
    return base[None, :] * factor


def shard_levels(stream_key, dims, split, smallest, largest):
    factor_of = 1.0
    for position, shards_of in split:
        heights = jax.random.uniform(jax.random.fold_in(jax.random.fold_in(stream_key, 6), position), (shards_of,), jnp.float32, smallest / len(split), largest / len(split))
        factor_of = factor_of * jnp.repeat(jnp.exp(heights), dims[position] // shards_of).reshape((-1,) + (1,) * (len(dims) - 1 - position))
    return factor_of


def bell_draw(key, shape, scale, reach, shards=(), kind=jnp.bfloat16):
    drawn = scale * jax.random.normal(key, shape, jnp.float32)
    if shards:
        drawn = drawn * shard_levels(key, shape, shards, -0.22, 0.18)
    return jnp.clip(drawn, -reach, reach).astype(kind)


def setup_inputs(seed: int = 0) -> dict:
    key_of = jax.random.split(jax.random.key(seed), 4)
    fields = draw_fields(jax.random.fold_in(key_of[3], 71), 0)
    conduct = draw_conduct(jax.random.fold_in(key_of[3], 71), 0)
    kernel = bell_draw(key_of[2], (NEAR, NAZ), NAZ ** -0.5, 0.1875, ((0, 8), (1, 16)), jnp.float32)
    return {"fields": fields, "conduct": conduct, "kernel": kernel}


def circular_filter(fields, kernel):
    near_cycles = fields[..., :NEAR]
    kernel_spectrum = jnp.fft.rfft(kernel, axis=1)
    near_spectrum = jnp.fft.rfft(near_cycles, axis=2)
    product = near_spectrum * jnp.transpose(kernel_spectrum)[None, None, :, :]
    return jnp.fft.irfft(product, n=NAZ, axis=2).astype(jnp.float32)

def reference(fields, conduct, kernel):
    filtered = jnp.concatenate([circular_filter(fields, kernel), fields[..., NEAR:]], axis=3)
    columns = NF * AXIAL
    right_side = jnp.transpose(filtered, (3, 2, 0, 1)).reshape(NR, NAZ, columns)
    faces = jnp.transpose(conduct)
    behind = jnp.roll(faces, 1, axis=1)
    zero_column = jnp.zeros((NR, 1), jnp.float32)
    lower_diag = jnp.concatenate([zero_column, -behind[:, 2:]], axis=1)
    upper_diag = jnp.concatenate([-faces[:, 1:NAZ - 1], zero_column], axis=1)
    main_diag = 1.0 + behind[:, 1:] + faces[:, 1:]
    couple = jnp.zeros((NR, NAZ - 1), jnp.float32)
    couple = couple.at[:, 0].add(-faces[:, 0])
    couple = couple.at[:, NAZ - 2].add(-faces[:, NAZ - 1])
    system = jnp.concatenate([right_side[:, 1:, :], couple[:, :, None]], axis=2)
    solved = lax.linalg.tridiagonal_solve(lower_diag, main_diag, upper_diag, system)
    inner_part = solved[:, :, :columns]
    spread = solved[:, :, columns:]
    low_sep = -faces[:, NAZ - 1]
    up_sep = -faces[:, 0]
    main_sep = 1.0 + faces[:, NAZ - 1] + faces[:, 0]
    numerator = right_side[:, 0, :] - up_sep[:, None] * inner_part[:, 0, :] - low_sep[:, None] * inner_part[:, NAZ - 2, :]
    denominator = main_sep - up_sep * spread[:, 0, 0] - low_sep * spread[:, NAZ - 2, 0]
    head_value = numerator / denominator[:, None]
    rest_values = inner_part - spread * head_value[:, None, :]
    assembled = jnp.concatenate([head_value[:, None, :], rest_values], axis=1)
    return jnp.transpose(assembled.reshape(NR, NAZ, NF, AXIAL), (2, 3, 1, 0))
```

```python
import functools

import jax
import jax.numpy as jnp
import ml_dtypes
import numpy as np
from jax import lax
from jax.experimental import pallas as pl
from jax.experimental.pallas import tpu as pltpu
from jax.sharding import PartitionSpec as P

MESH = pl.DeviceIdType.MESH
F32 = jnp.float32
BF16 = jnp.bfloat16

NF = 3
NX = 8
NB = 64
NQ = 16
HALF = NB * NQ // 2
NEAR = 128
FAR_TILES = 3
FAR = NF * FAR_TILES
OFFSETS = (0, 32, 48, 56, 60, 62)
ORDER = (8, 4, 12, 1, 9, 5, 13, 2, 10, 6, 14, 3, 11, 7, 15)


def split_const(matrix):
    high = matrix.astype(ml_dtypes.bfloat16)
    low = (matrix - high.astype(np.float64)).astype(ml_dtypes.bfloat16)
    return high, low


def transforms():
    points = 2 * HALF
    j = np.arange(HALF)
    forward, inverse = [], []
    for odd in (0, 1):
        freq = 2 * np.arange(HALF // 2) + odd
        angle = 2.0 * np.pi * ((freq[:, None] * j[None, :]) % points) / points
        real, imag = np.cos(angle), -np.sin(angle)
        scale = np.full((HALF // 2, 1), 2.0 / points)
        real_back, imag_back = real * scale, imag * scale
        if not odd:
            imag[0] = np.cos(np.pi * j)
            real_back[0] = 1.0 / points
            imag_back[0] = imag[0] / points
        forward.append(np.concatenate([real, imag]))
        inverse.append(np.concatenate([real_back, imag_back]))
    order = (NB * np.arange(8)[None, :] + np.arange(NB)[:, None]).reshape(-1)
    back = np.concatenate(inverse, axis=0).T[order]
    even_high, even_low = split_const(forward[0])
    odd_high, odd_low = split_const(forward[1])
    back_high, back_low = split_const(back)
    return np.stack([even_high, even_low, odd_high, odd_low]), np.stack([back_high, back_low])


def split(x):
    high = x.astype(BF16)
    return high, (x - high.astype(F32)).astype(BF16)


def forward_transform(dft_ref, which, rows):
    high, low = split(rows)
    both = jnp.concatenate([high, low], axis=0)
    contract = (((1,), (1,)), ((), ()))
    one = lax.dot_general(dft_ref[2 * which], both, contract, preferred_element_type=F32)
    two = lax.dot_general(dft_ref[2 * which + 1], high, contract, preferred_element_type=F32)
    return one[:, :128] + one[:, 128:] + two


def inverse_transform(idft_ref, spectrum):
    high, low = split(spectrum)
    both = jnp.concatenate([high, low], axis=1)
    contract = (((1,), (0,)), ((), ()))
    one = lax.dot_general(idft_ref[0], both, contract, preferred_element_type=F32)
    two = lax.dot_general(idft_ref[1], high, contract, preferred_element_type=F32)
    return one[:, :128] + one[:, 128:] + two


def coefficients(links, store):
    excess = jnp.ones(links.shape, F32)
    onward = None
    for level in range(6):
        count = links.shape[0] // 2
        pairs = links.reshape(count, 2, 8, 128)
        behind, ahead = pairs[:, 0], pairs[:, 1]
        own = excess.reshape(count, 2, 8, 128)
        inv = 1.0 / (behind + ahead + own[:, 1])
        alpha, beta = behind * inv, ahead * inv
        store(OFFSETS[level], alpha, beta, inv)
        to_left, to_right = alpha * own[:, 1], beta * own[:, 1]
        excess = own[:, 0] + to_left
        if count > 1:
            excess = jnp.concatenate([excess[:1], excess[1:] + to_right[:-1]], axis=0)
        onward = to_right[count - 1] if onward is None else onward + to_right[count - 1]
        links = behind * beta
    return links[0], excess[0], onward


def reduce_block(values, load, keep):
    onward = None
    for level in range(6):
        count = values.shape[0] // 2
        pairs = values.reshape(count, 2, 8, 128)
        even, odd = pairs[:, 0], pairs[:, 1]
        keep(OFFSETS[level], odd)
        alpha, beta, _ = load(OFFSETS[level], count)
        to_right = beta * odd
        values = even + alpha * odd
        if count > 1:
            values = jnp.concatenate([values[:1], values[1:] + to_right[:-1]], axis=0)
        onward = to_right[count - 1] if onward is None else onward + to_right[count - 1]
    return values[0], onward


def expand_block(first, following, load, kept):
    solved = first[None]
    for level in reversed(range(6)):
        count = 32 >> level
        alpha, beta, inv = load(OFFSETS[level], count)
        right = following[None]
        if count > 1:
            right = jnp.concatenate([solved[1:], right], axis=0)
        odd = inv * kept(OFFSETS[level], count) + alpha * solved + beta * right
        solved = jnp.stack([solved, odd], axis=1).reshape(2 * count, 8, 128)
    return solved


def ring_coefficients(link, first, onward, prev, ahead):
    excess = first + prev(onward, 1)
    after, before = link, prev(link, 1)
    levels = []
    for d in (1, 2, 4, 8):
        inv = 1.0 / (excess + before + after)
        alpha, beta = before * prev(inv, d), after * ahead(inv, d)
        levels.append((alpha, beta))
        excess = excess + alpha * prev(excess, d) + beta * ahead(excess, d)
        if d < 8:
            before, after = alpha * prev(before, d), beta * ahead(after, d)
    return levels, 1.0 / excess


def ring_solve(first, onward, levels, final, prev, ahead):
    value = first + prev(onward, 1)
    for d, (alpha, beta) in zip((1, 2, 4, 8), levels):
        value = value + alpha * prev(value, d) + beta * ahead(value, d)
    return value * final


def far_prev(v, d):
    return jnp.concatenate([v[NQ - d :], v[: NQ - d]], axis=0)


def far_ahead(v, d):
    return jnp.concatenate([v[d:], v[:d]], axis=0)


def near_prev(v, d):
    if d == 8:
        return pltpu.roll(v, 64, 1)
    rolled = pltpu.roll(v, d, 0)
    row = lax.broadcasted_iota(jnp.int32, (8, 128), 0)
    return jnp.where(row >= d, rolled, pltpu.roll(rolled, 64, 1))


def near_ahead(v, d):
    if d == 8:
        return pltpu.roll(v, 64, 1)
    rolled = pltpu.roll(v, 8 - d, 0)
    row = lax.broadcasted_iota(jnp.int32, (8, 128), 0)
    return jnp.where(row < 8 - d, rolled, pltpu.roll(rolled, 64, 1))


def swap_halves(x):
    return pltpu.roll(x, 64, x.ndim - 1)


def kernel_body(
    fields, conduct, kernel, dft, idft, out,
    held, done, dft_v, idft_v, near_send, near_recv, back_send, back_recv,
    kernel_pad, kernel_recv, conduct_send, conduct_recv, link_rows, spectrum,
    alpha_ref, beta_ref, inv_ref, ring_ref, odd_ref, work,
    far_send, far_recv, sep_send, sep_recv,
    load_sem, const_sem, store_sem, ns, nr, bs, br, ks, kr, cs, cr, fs, fr, ss, sr,
):
    me = lax.axis_index("az")
    mx = lax.axis_index("ax")
    blocks = kernel.shape[0] // 8
    ax_count = lax.axis_size("ax")
    my_group = me // blocks

    def peer(k):
        return lax.rem(me + k, NQ)

    def source(k):
        return lax.rem(me + NQ - k, NQ)

    loads = {}
    for tile in range(4):
        for f in range(NF):
            copy = pltpu.make_async_copy(
                fields.at[f, :, pl.ds(128 * tile, 128)], held.at[f * 4 + tile], load_sem.at[f * 4 + tile]
            )
            loads[f, tile] = copy
            if tile == 0:
                copy.start()
    const_loads = [
        pltpu.make_async_copy(dft, dft_v, const_sem.at[0]),
        pltpu.make_async_copy(idft, idft_v, const_sem.at[1]),
    ]

    barrier = pltpu.get_barrier_semaphore()
    for k in ORDER:
        pl.semaphore_signal(barrier, inc=1, device_id={"az": peer(k), "ax": mx}, device_id_type=MESH)
    for k in range(1, NQ):
        pl.semaphore_signal(barrier, inc=1, device_id={"az": peer(k), "ax": my_group}, device_id_type=MESH)

    @pl.when(my_group != mx)
    def _():
        pl.semaphore_signal(barrier, inc=1, device_id={"az": me, "ax": my_group}, device_id_type=MESH)

    for copy in const_loads:
        copy.start()
    for tile in range(1, 4):
        for f in range(NF):
            loads[f, tile].start()

    kernel_pad[...] = jnp.concatenate([kernel[...], jnp.zeros(kernel.shape, F32)], axis=1).reshape(blocks, 8, 128)
    near_links = conduct[:, :NEAR]
    conduct_send[...] = jnp.concatenate([near_links, near_links], axis=0).T.reshape(NQ, 8, 128)
    conduct_recv[me] = conduct_send[me]

    def transpose_near(f):
        loads[f, 0].wait()
        for k in range(4):
            near_send[f, :, k] = held[f * 4, 128 * k : 128 * k + 128, :].T.reshape(NQ, 8, 128)
        near_recv[f, me] = near_send[f, me]

    transpose_near(0)

    incoming = 15 + blocks * ax_count - jnp.where(my_group == mx, 1, 0)
    pl.semaphore_wait(barrier, incoming)

    def kernel_copy(b, dq):
        return pltpu.make_async_remote_copy(
            kernel_pad.at[b], kernel_recv.at[me], ks.at[b, dq], kr.at[me],
            device_id={"az": blocks * mx + b, "ax": lax.rem(mx + dq, ax_count)}, device_id_type=MESH,
        )

    for b in range(blocks):
        for dq in range(ax_count):
            if dq:
                kernel_copy(b, dq).start()
            else:

                @pl.when(me == blocks * mx + b)
                def _():
                    kernel_recv[me] = kernel_pad[b]

                @pl.when(me != blocks * mx + b)
                def _():
                    kernel_copy(b, 0).start()

    def near_copy(f, k, slot):
        return pltpu.make_async_remote_copy(
            near_send.at[f, peer(k)], near_recv.at[f, slot], ns.at[f, k], nr.at[f, k],
            device_id={"az": peer(k), "ax": mx}, device_id_type=MESH,
        )

    def conduct_copy(k, slot):
        return pltpu.make_async_remote_copy(
            conduct_send.at[peer(k)], conduct_recv.at[slot], cs.at[k], cr.at[k],
            device_id={"az": peer(k), "ax": mx}, device_id_type=MESH,
        )

    for k in ORDER:
        near_copy(0, k, me).start()
    for k in ORDER:
        conduct_copy(k, me).start()
    for f in (1, 2):
        transpose_near(f)
        for k in ORDER:
            near_copy(f, k, me).start()

    def coefficient_store(c):
        def store(offset, alpha, beta, inv):
            count = alpha.shape[0]
            alpha_ref[c, offset : offset + count] = alpha
            beta_ref[c, offset : offset + count] = beta
            inv_ref[c, offset : offset + count] = inv

        return store

    def coefficient_load(c):
        def load(offset, count):
            return (
                alpha_ref[c, offset : offset + count],
                beta_ref[c, offset : offset + count],
                inv_ref[c, offset : offset + count],
            )

        return load

    def odd_keep(w):
        def keep(offset, value):
            odd_ref[w, offset : offset + value.shape[0]] = value

        return keep

    def odd_load(w):
        return lambda offset, count: odd_ref[w, offset : offset + count]

    row = lax.broadcasted_iota(jnp.int32, (8, 128), 0)

    def far_coefficients(lt, carry):
        lanes = pl.ds(pl.multiple_of(128 * lt + NEAR, 128), 128)
        links = jnp.stack([jnp.broadcast_to(conduct[j : j + 1, lanes], (8, 128)) for j in range(NB)])
        link, first, onward = coefficients(links, coefficient_store(lt + 1))
        tile = jnp.where(row == 0, link, jnp.where(row == 1, first, onward))
        for f in range(NF):
            far_send[f * FAR_TILES + lt, 2] = tile
        return carry

    lax.fori_loop(0, FAR_TILES, far_coefficients, 0)

    for f in range(NF):
        for tile in range(1, 4):
            loads[f, tile].wait()

    def far_index(w):
        return w // FAR_TILES, lax.rem(w, FAR_TILES)

    def far_reduce(w, carry):
        f, lt = far_index(w)
        values = jnp.stack([held[f * 4 + lt + 1, pl.ds(j, 8, stride=NB), :] for j in range(NB)])
        first, onward = reduce_block(values, coefficient_load(lt + 1), odd_keep(w))
        far_send[w, 0] = first
        far_send[w, 1] = onward
        return carry

    lax.fori_loop(0, FAR, far_reduce, 0)

    def owner(w):
        return 2 * w if w < 8 else 1

    def far_copy(w):
        return pltpu.make_async_remote_copy(
            far_send.at[w], far_recv.at[me], fs.at[w], fr.at[me],
            device_id={"az": owner(w), "ax": mx}, device_id_type=MESH,
        )

    for w in range(FAR):

        @pl.when(me == owner(w))
        def _():
            far_recv[me] = far_send[w]

        @pl.when(me != owner(w))
        def _():
            far_copy(w).start()

    for k in range(NQ):

        def wait_kernel():
            pltpu.make_async_remote_copy(
                kernel_pad.at[0], kernel_recv.at[source(k)], ks.at[0, 0], kr.at[source(k)],
                device_id={"az": source(k), "ax": my_group}, device_id_type=MESH,
            ).wait_recv()

        if k:
            wait_kernel()
        else:
            pl.when(my_group != mx)(wait_kernel)
    for copy in const_loads:
        copy.wait()

    lane = lax.broadcasted_iota(jnp.int32, (8, 128), 1)
    pieces = kernel_recv[...].reshape(8, 2, 8, 128)
    lags = jnp.where(lane[None] < 64, pieces[:, 0], swap_halves(pieces[:, 1].reshape(64, 128)).reshape(8, 8, 128))
    total, difference = lags[:4] + lags[4:], lags[:4] - lags[4:]
    for odd, part in enumerate((total, difference)):
        rows = jnp.concatenate([part[m] for m in range(4)], axis=1)
        rows = jnp.concatenate([rows] * 16, axis=0)
        transformed = forward_transform(dft_v, odd, rows)
        real, imag = transformed[:256], transformed[256:]
        if odd:
            spectrum[3] = real
            spectrum[4] = imag
        else:
            first_row = lax.broadcasted_iota(jnp.int32, (256, 128), 0) == 0
            spectrum[0] = real
            spectrum[1] = jnp.where(first_row, 0.0, imag)
            spectrum[2] = jnp.where(first_row, imag, real)

    for k in ORDER:
        conduct_copy(k, source(k)).wait_recv()
    for s in range(8):
        rows = jnp.concatenate([conduct_recv[s]] * 8 + [conduct_recv[8 + s]] * 8, axis=0)
        link_rows[pl.ds(s, NB, stride=8), :] = rows.T[:NB]
    link, first, onward = coefficients(link_rows[...].reshape(NB, 8, 128), coefficient_store(0))
    levels, final = ring_coefficients(link, first, onward, near_prev, near_ahead)
    for index, (alpha, beta) in enumerate(levels):
        ring_ref[2 * index] = alpha
        ring_ref[2 * index + 1] = beta
    ring_ref[8] = final

    def back_copy(f, k, slot):
        return pltpu.make_async_remote_copy(
            back_send.at[f, peer(k)], back_recv.at[f, :, slot], bs.at[f, k], br.at[f, k],
            device_id={"az": peer(k), "ax": mx}, device_id_type=MESH,
        )

    def near_solve(f):
        for k in ORDER:
            near_copy(f, k, source(k)).wait_recv()
        pieces = near_recv[f].reshape(8, 2, 4, 8, 128)
        low, high = pieces[:, 0].reshape(256, 128), pieces[:, 1].reshape(256, 128)
        left = lax.broadcasted_iota(jnp.int32, (256, 128), 1) < 64
        plane_a = jnp.where(left, low, swap_halves(high)).reshape(8, 4, 8, 128)
        plane_b = jnp.where(left, swap_halves(low), high).reshape(8, 4, 8, 128)
        points = jnp.stack([plane_a, plane_b], axis=2).reshape(8, 64, 128)
        total, difference = points[:4] + points[4:], points[:4] - points[4:]
        total = jnp.concatenate([total[m] for m in range(4)], axis=1)
        difference = jnp.concatenate([difference[m] for m in range(4)], axis=1)
        even = forward_transform(dft_v, 0, jnp.concatenate([total, total], axis=0))
        odd = forward_transform(dft_v, 1, jnp.concatenate([difference, -difference], axis=0))
        real, imag = even[:256], even[256:]
        odd_real, odd_imag = odd[:256], odd[256:]
        product = jnp.concatenate(
            [
                real * spectrum[0] - imag * spectrum[1],
                real * spectrum[1] + imag * spectrum[2],
                odd_real * spectrum[3] - odd_imag * spectrum[4],
                odd_real * spectrum[4] + odd_imag * spectrum[3],
            ],
            axis=0,
        )
        filtered = inverse_transform(idft_v, product).reshape(NB, 8, 128)
        first, onward = reduce_block(filtered, coefficient_load(0), odd_keep(FAR))
        ring = [(ring_ref[2 * i], ring_ref[2 * i + 1]) for i in range(4)]
        first = ring_solve(first, onward, ring, ring_ref[8], near_prev, near_ahead)
        solved = expand_block(first, near_ahead(first, 1), coefficient_load(0), odd_load(FAR))
        work[...] = solved.reshape(512, 128)
        for s in range(8):
            part = work[pl.ds(s, NB, stride=8), :]
            tiles = jnp.concatenate([part, pltpu.roll(part, 120, 1)], axis=0).T
            tiles = tiles.reshape(2, 4, 2, 8, 128)[:, :, 0]
            back_send[f, s] = tiles[0]
            back_send[f, 8 + s] = tiles[1]
        back_recv[f, :, me] = back_send[f, me]
        for k in ORDER:
            back_copy(f, k, me).start()

    sep_owner = jnp.logical_or(lax.rem(me, 2) == 0, me == 1)
    my_item = jnp.where(me == 1, 8, me // 2)

    def sep_copy(k, w):
        return pltpu.make_async_remote_copy(
            sep_send.at[peer(k)], sep_recv.at[w], ss.at[k], sr.at[w],
            device_id={"az": peer(k), "ax": mx}, device_id_type=MESH,
        )

    def far_ring():
        for k in range(1, NQ):
            pltpu.make_async_remote_copy(
                far_send.at[0], far_recv.at[source(k)], fs.at[0], fr.at[source(k)],
                device_id={"az": source(k), "ax": mx}, device_id_type=MESH,
            ).wait_recv()
        spread = [jnp.broadcast_to(far_recv[:, 2, i : i + 1, :], (NQ, 8, 128)) for i in range(3)]
        levels, final = ring_coefficients(*spread, far_prev, far_ahead)
        value = ring_solve(far_recv[:, 0], far_recv[:, 1], levels, final, far_prev, far_ahead)
        sep_send[:, 0] = value
        sep_send[:, 1] = far_ahead(value, 1)
        sep_recv[my_item] = sep_send[me]
        for k in ORDER:
            sep_copy(k, my_item).start()

    stores = {}
    for f in range(NF):
        for tile in range(4):
            stores[f, tile] = pltpu.make_async_copy(
                done.at[f * 4 + tile], out.at[f, :, pl.ds(128 * tile, 128)], store_sem.at[f * 4 + tile]
            )

    near_solve(0)
    pl.when(sep_owner)(far_ring)
    near_solve(1)

    for w in range(FAR):

        @pl.when(me != owner(w))
        def _():
            pltpu.make_async_remote_copy(
                sep_send.at[0], sep_recv.at[w], ss.at[0], sr.at[w],
                device_id={"az": owner(w), "ax": mx}, device_id_type=MESH,
            ).wait_recv()

    def far_expand(w, carry):
        f, lt = far_index(w)
        solved = expand_block(sep_recv[w, 0], sep_recv[w, 1], coefficient_load(lt + 1), odd_load(w))
        for j in range(NB):
            done[f * 4 + lt + 1, pl.ds(j, 8, stride=NB), :] = solved[j]
        return carry

    lax.fori_loop(0, FAR, far_expand, 0)
    for f in range(NF):
        for tile in range(1, 4):
            stores[f, tile].start()

    near_solve(2)

    for f in range(NF):
        for k in ORDER:
            back_copy(f, k, source(k)).wait_recv()
        for k in range(4):
            done[f * 4, 128 * k : 128 * k + 128, :] = back_recv[f, k].reshape(128, 128).T
        stores[f, 0].start()

    for b in range(blocks):
        for dq in range(ax_count):
            if dq:
                kernel_copy(b, dq).wait_send()
            else:

                @pl.when(me != blocks * mx + b)
                def _():
                    kernel_copy(b, 0).wait_send()

    for k in ORDER:
        conduct_copy(k, me).wait_send()
        for f in range(NF):
            near_copy(f, k, me).wait_send()
            back_copy(f, k, me).wait_send()
    for w in range(FAR):

        @pl.when(me != owner(w))
        def _():
            far_copy(w).wait_send()

    @pl.when(sep_owner)
    def _():
        for k in ORDER:
            sep_copy(k, my_item).wait_send()

    for copy in stores.values():
        copy.wait()


def body(fields, conduct, kernel):
    dft, idft = transforms()
    shape = fields.shape
    flat = fields.reshape(NF, NX * NB, shape[3])
    blocks = kernel.shape[0] // 8
    vmem = pltpu.VMEM
    dma = pltpu.SemaphoreType.DMA
    anywhere = pl.BlockSpec(memory_space=pl.ANY)
    inside = pl.BlockSpec(memory_space=pltpu.VMEM)
    out = pl.pallas_call(
        kernel_body,
        out_shape=jax.ShapeDtypeStruct(flat.shape, F32),
        in_specs=[anywhere, inside, inside, anywhere, anywhere],
        out_specs=anywhere,
        scratch_shapes=[
            vmem((12, 512, 128), F32),
            vmem((12, 512, 128), F32),
            vmem((4, 512, 512), BF16),
            vmem((2, 512, 1024), BF16),
            vmem((NF, NQ, 4, 8, 128), F32),
            vmem((NF, NQ, 4, 8, 128), F32),
            vmem((NF, NQ, 4, 8, 128), F32),
            vmem((NF, 4, NQ, 8, 128), F32),
            vmem((blocks, 8, 128), F32),
            vmem((NQ, 8, 128), F32),
            vmem((NQ, 8, 128), F32),
            vmem((NQ, 8, 128), F32),
            vmem((512, 128), F32),
            vmem((5, 256, 128), F32),
            vmem((4, 64, 8, 128), F32),
            vmem((4, 64, 8, 128), F32),
            vmem((4, 64, 8, 128), F32),
            vmem((9, 8, 128), F32),
            vmem((FAR + 1, 64, 8, 128), F32),
            vmem((512, 128), F32),
            vmem((FAR, 3, 8, 128), F32),
            vmem((NQ, 3, 8, 128), F32),
            vmem((NQ, 2, 8, 128), F32),
            vmem((FAR, 2, 8, 128), F32),
            dma((12,)), dma((2,)), dma((12,)),
            dma((NF, NQ)), dma((NF, NQ)), dma((NF, NQ)), dma((NF, NQ)),
            dma((blocks, lax.axis_size("ax"))), dma((NQ,)),
            dma((NQ,)), dma((NQ,)),
            dma((FAR,)), dma((NQ,)),
            dma((NQ,)), dma((FAR,)),
        ],
        compiler_params=pltpu.CompilerParams(
            collective_id=0, has_side_effects=True, vmem_limit_bytes=50 * 2**20
        ),
    )(flat, conduct, kernel, jnp.asarray(dft), jnp.asarray(idft))
    return out.reshape(shape)


def solution(mesh):
    return jax.shard_map(
        body,
        mesh=mesh,
        in_specs=(P(None, "ax", "az", None), P("az", None), P("ax", "az")),
        out_specs=P(None, "ax", "az", None),
        check_vma=False,
    )
```

```python
import functools

import jax
import jax.numpy as jnp
import numpy as np
from jax import lax
from jax.experimental import pallas as pl
from jax.experimental.pallas import tpu as pltpu
from jax.sharding import PartitionSpec as P

MESH = pl.DeviceIdType.MESH
F32 = jnp.float32
BF16 = jnp.bfloat16

NF = 3
NX = 8
NB = 64
NQ = 16
HALF = NB * NQ // 2
NEAR = 128
FAR_TILES = 3
FAR = NF * FAR_TILES
MEMBERS = 4
SLICES = NQ // MEMBERS
SLOTS = 3
NEAR_STEPS = (1, 2, 4, 8)
FAR_STEPS = (1, 2)


def transforms():
    points = 2 * HALF
    j = np.arange(HALF)
    forward, inverse = [], []
    for odd in (0, 1):
        freq = 2 * np.arange(HALF // 2) + odd
        angle = 2.0 * np.pi * ((freq[:, None] * j[None, :]) % points) / points
        real, imag = np.cos(angle), -np.sin(angle)
        scale = np.full((HALF // 2, 1), 2.0 / points)
        real_back, imag_back = real * scale, imag * scale
        if not odd:
            imag[0] = np.cos(np.pi * j)
            real_back[0] = 1.0 / points
            imag_back[0] = imag[0] / points
        forward.append(np.concatenate([real, imag]))
        inverse.append(np.concatenate([real_back, imag_back]))
    order = (NB * np.arange(8)[None, :] + np.arange(NB)[:, None]).reshape(-1)
    back = np.concatenate(inverse, axis=0).T[order]
    return np.stack(forward).astype(np.float32), back.astype(np.float32)


def split(x):
    high = x.astype(BF16)
    return high, (x - high.astype(F32)).astype(BF16)


def forward_transform(dft_ref, which, rows):
    high, low = split(rows)
    both = jnp.concatenate([high, low], axis=0)
    contract = (((1,), (1,)), ((), ()))
    one = lax.dot_general(dft_ref[2 * which], both, contract, preferred_element_type=F32)
    two = lax.dot_general(dft_ref[2 * which + 1], high, contract, preferred_element_type=F32)
    return one[:, :128] + one[:, 128:] + two


def inverse_transform(idft_ref, spectrum):
    high, low = split(spectrum)
    both = jnp.concatenate([high, low], axis=1)
    contract = (((1,), (0,)), ((), ()))
    one = lax.dot_general(idft_ref[0], both, contract, preferred_element_type=F32)
    two = lax.dot_general(idft_ref[1], high, contract, preferred_element_type=F32)
    return one[:, :128] + one[:, 128:] + two


def place(count):
    return NB - 2 * count


def coefficients(links, excess, onward, store):
    while links.shape[0] > 1:
        count = links.shape[0] // 2
        pairs = links.reshape(count, 2, 8, 128)
        behind, ahead = pairs[:, 0], pairs[:, 1]
        own = excess.reshape(count, 2, 8, 128)
        inv = 1.0 / (behind + ahead + own[:, 1])
        alpha, beta = behind * inv, ahead * inv
        store(place(count), alpha, beta, inv)
        to_left, to_right = alpha * own[:, 1], beta * own[:, 1]
        excess = own[:, 0] + to_left
        if count > 1:
            excess = jnp.concatenate([excess[:1], excess[1:] + to_right[:-1]], axis=0)
        onward = to_right[count - 1] if onward is None else onward + to_right[count - 1]
        links = behind * beta
    return links[0], excess[0], onward


def reduce_block(values, onward, load, keep):
    while values.shape[0] > 1:
        count = values.shape[0] // 2
        pairs = values.reshape(count, 2, 8, 128)
        even, odd = pairs[:, 0], pairs[:, 1]
        keep(place(count), odd)
        alpha, beta, _ = load(place(count), count)
        to_right = beta * odd
        values = even + alpha * odd
        if count > 1:
            values = jnp.concatenate([values[:1], values[1:] + to_right[:-1]], axis=0)
        onward = to_right[count - 1] if onward is None else onward + to_right[count - 1]
    return values[0], onward


def expand_block(first, following, length, load, kept):
    solved = first[None]
    while solved.shape[0] < length:
        count = solved.shape[0]
        alpha, beta, inv = load(place(count), count)
        right = following[None]
        if count > 1:
            right = jnp.concatenate([solved[1:], right], axis=0)
        odd = inv * kept(place(count), count) + alpha * solved + beta * right
        solved = jnp.stack([solved, odd], axis=1).reshape(2 * count, 8, 128)
    return solved


def ring_coefficients(link, first, onward, steps, prev, ahead):
    excess = first + prev(onward, 1)
    after, before = link, prev(link, 1)
    levels = []
    for d in steps:
        inv = 1.0 / (excess + before + after)
        alpha, beta = before * prev(inv, d), after * ahead(inv, d)
        levels.append((alpha, beta))
        excess = excess + alpha * prev(excess, d) + beta * ahead(excess, d)
        if d < steps[-1]:
            before, after = alpha * prev(before, d), beta * ahead(after, d)
    return levels, 1.0 / excess


def ring_solve(first, onward, levels, final, steps, prev, ahead):
    value = first + prev(onward, 1)
    for d, (alpha, beta) in zip(steps, levels):
        value = value + alpha * prev(value, d) + beta * ahead(value, d)
    return value * final


def far_prev(v, d):
    return jnp.concatenate([v[-d:], v[:-d]], axis=0)


def far_ahead(v, d):
    return jnp.concatenate([v[d:], v[:d]], axis=0)


def near_prev(v, d):
    if d == 8:
        return pltpu.roll(v, 64, 1)
    rolled = pltpu.roll(v, d, 0)
    row = lax.broadcasted_iota(jnp.int32, (8, 128), 0)
    return jnp.where(row >= d, rolled, pltpu.roll(rolled, 64, 1))


def near_ahead(v, d):
    if d == 8:
        return pltpu.roll(v, 64, 1)
    rolled = pltpu.roll(v, 8 - d, 0)
    row = lax.broadcasted_iota(jnp.int32, (8, 128), 0)
    return jnp.where(row < 8 - d, rolled, pltpu.roll(rolled, 64, 1))


def swap_halves(x):
    return pltpu.roll(x, 64, x.ndim - 1)


def each(count, step):
    def run(i, carry):
        step(i)
        return carry

    lax.fori_loop(0, count, run, 0)


def offset(i):
    n = i + 1
    return 8 * lax.rem(n, 2) + 4 * lax.rem(n // 2, 2) + 2 * lax.rem(n // 4, 2) + n // 8


def kernel_body(
    fields, conduct_hbm, kernel_hbm, dft, idft, out,
    held, conduct, kernel, dft_raw, idft_raw, dft_v, idft_v, near_send, near_recv, back_send, back_recv,
    kernel_all, links_send, links_recv, link_rows, rows_ref, freq_ref, spectrum,
    alpha_ref, beta_ref, inv_ref, ring_ref, odd_ref, work,
    far_send, far_recv, slice_send, slice_recv, ring_values, sep_send, sep_recv,
    load_sem, const_sem, ns, nr, bs, br, ks, kr, cs, cr, fs, fr, xs, xr, ss, sr,
):
    me = lax.axis_index("az")
    mx = lax.axis_index("ax")
    ax_count = lax.axis_size("ax")
    member, section = lax.rem(me, MEMBERS), me // MEMBERS
    others = NQ - 1

    def peer(k):
        return lax.rem(me + k, NQ)

    def plane(k):
        return lax.rem(mx + k, ax_count)

    def mate(k):
        return lax.rem(member + k, MEMBERS)

    def remote(src, dst, send, recv, az, ax):
        return pltpu.make_async_remote_copy(
            src, dst, send, recv, device_id={"az": az, "ax": ax}, device_id_type=MESH
        )

    barrier = pltpu.get_barrier_semaphore()

    @functools.partial(each, others)
    def _(i):
        pl.semaphore_signal(barrier, inc=1, device_id={"az": peer(offset(i)), "ax": mx}, device_id_type=MESH)

    @functools.partial(each, ax_count - 1)
    def _(i):
        pl.semaphore_signal(barrier, inc=1, device_id={"az": me, "ax": plane(i + 1)}, device_id_type=MESH)

    def load(f, tile):
        return pltpu.make_async_copy(
            fields.at[f, :, pl.ds(pl.multiple_of(128 * tile, 128), 128)], held.at[f * 4 + tile], load_sem.at[f * 4 + tile]
        )

    small_loads = [
        pltpu.make_async_copy(kernel_hbm, kernel, const_sem.at[2]),
        pltpu.make_async_copy(conduct_hbm, conduct, const_sem.at[3]),
    ]
    const_loads = [
        pltpu.make_async_copy(dft, dft_raw, const_sem.at[0]),
        pltpu.make_async_copy(idft, idft_raw, const_sem.at[1]),
    ]
    each(NF, lambda f: load(f, 0).start())
    for copy in small_loads:
        copy.start()
    each(NF * FAR_TILES, lambda i: load(i // FAR_TILES, lax.rem(i, FAR_TILES) + 1).start())
    for copy in const_loads:
        copy.start()

    def transpose_near(f):
        load(f, 0).wait()

        @functools.partial(each, 4)
        def _(k):
            part = held[f * 4, pl.ds(pl.multiple_of(128 * k, 128), 128), :]
            near_send[f, :, k] = part.T.reshape(NQ, 8, 128)

        near_recv[f, me] = near_send[f, me]

    transpose_near(0)
    for copy in small_loads:
        copy.wait()
    kernel_all[mx] = jnp.concatenate([kernel[0:8, :], kernel[8:16, :]], axis=1)

    pl.semaphore_wait(barrier, others + ax_count - 1)

    @functools.partial(each, ax_count - 1)
    def _(i):
        remote(kernel_all.at[mx], kernel_all.at[mx], ks, kr, me, plane(i + 1)).start()

    kernel_whole = kernel_all.at[pl.ds(0, ax_count - 1)]
    kernel_wait = remote(kernel_whole, kernel_whole, ks, kr, me, plane(1))

    def send_near(f):
        @functools.partial(each, others)
        def _(i):
            k = peer(offset(i))
            remote(near_send.at[f, k], near_recv.at[f, me], ns.at[f], nr.at[f], k, mx).start()

    def near_wait(f):
        whole = pl.ds(0, others)
        return remote(near_send.at[f, whole], near_recv.at[f, whole], ns.at[f], nr.at[f], peer(1), mx)

    send_near(0)

    row = lax.broadcasted_iota(jnp.int32, (8, 128), 0)
    lane = lax.broadcasted_iota(jnp.int32, (8, 128), 1)
    near_links = conduct[:, :NEAR]
    near_links = jnp.concatenate([near_links, near_links], axis=0).T.reshape(NQ, 8, 128)
    kernel_wait.wait_recv()
    kernels = kernel_all[...]
    swapped = swap_halves(kernels.reshape(64, 128)).reshape(8, 8, 128)
    kernels = jnp.stack([swapped, kernels], axis=1).reshape(NQ, 8, 128)
    links_send[...] = jnp.where(lane[None] < 64, near_links, kernels)
    links_recv[me] = links_send[me]

    @functools.partial(each, others)
    def _(i):
        k = peer(offset(i))
        remote(links_send.at[k], links_recv.at[me], cs, cr, k, mx).start()

    links_wait = remote(links_send.at[pl.ds(0, others)], links_recv.at[pl.ds(0, others)], cs, cr, peer(1), mx)
    transpose_near(1)
    send_near(1)
    transpose_near(2)

    def coefficient_store(c):
        def store(offset, alpha, beta, inv):
            count = alpha.shape[0]
            alpha_ref[c, offset : offset + count] = alpha
            beta_ref[c, offset : offset + count] = beta
            inv_ref[c, offset : offset + count] = inv

        return store

    def coefficient_load(c):
        def load(offset, count):
            return (
                alpha_ref[c, offset : offset + count],
                beta_ref[c, offset : offset + count],
                inv_ref[c, offset : offset + count],
            )

        return load

    def odd_keep(w):
        def keep(offset, value):
            odd_ref[w, offset : offset + value.shape[0]] = value

        return keep

    def odd_load(w):
        return lambda offset, count: odd_ref[w, offset : offset + count]

    unit = jnp.ones((NB, 8, 128), F32)

    def packed(link, first, onward):
        return jnp.where(row == 0, link, jnp.where(row == 1, first, onward))

    @functools.partial(each, FAR_TILES)
    def _(lt):
        lanes = pl.ds(pl.multiple_of(128 * lt + NEAR, 128), 128)
        links = jnp.stack([jnp.broadcast_to(conduct[j : j + 1, lanes], (8, 128)) for j in range(NB)])
        tile = packed(*coefficients(links, unit, None, coefficient_store(lt + 1)))
        for f in range(NF):
            far_send[f * FAR_TILES + lt, 2] = tile

    each(NF * FAR_TILES, lambda i: load(i // FAR_TILES, lax.rem(i, FAR_TILES) + 1).wait())

    @functools.partial(each, FAR)
    def _(w):
        f, lt = w // FAR_TILES, lax.rem(w, FAR_TILES)
        values = jnp.stack([held[f * 4 + lt + 1, pl.ds(j, 8, stride=NB), :] for j in range(NB)])
        first, onward = reduce_block(values, None, coefficient_load(lt + 1), odd_keep(w))
        far_send[w, 0] = first
        far_send[w, 1] = onward

    @functools.partial(each, FAR)
    def _(w):
        slot, owner = w // MEMBERS, lax.rem(w, MEMBERS)

        @pl.when(member == owner)
        def _():
            far_recv[slot, member] = far_send[w]

        @pl.when(member != owner)
        def _():
            remote(
                far_send.at[w], far_recv.at[slot, member], fs.at[slot], fr.at[slot], MEMBERS * section + owner, mx
            ).start()

    def far_wait(slot, count):
        return remote(
            far_send.at[pl.ds(0, count)], far_recv.at[slot, pl.ds(0, count)], fs.at[slot], fr.at[slot],
            MEMBERS * section + mate(1), mx,
        )

    send_near(2)

    def far_section(slot):
        far_wait(slot, MEMBERS - 1).wait_recv()
        shape = (MEMBERS, 8, 128)
        link, first, onward = [jnp.broadcast_to(far_recv[slot, :, 2, i : i + 1, :], shape) for i in range(3)]
        first = jnp.concatenate([first[:1], first[1:] + onward[:-1]], axis=0)
        tile = packed(*coefficients(link, first, onward[MEMBERS - 1], coefficient_store(4 + slot)))
        values, onward = far_recv[slot, :, 0], far_recv[slot, :, 1]
        values = jnp.concatenate([values[:1], values[1:] + onward[:-1]], axis=0)
        value, onward = reduce_block(values, onward[MEMBERS - 1], coefficient_load(4 + slot), odd_keep(FAR + 1 + slot))
        slice_send[slot, 0] = value
        slice_send[slot, 1] = onward
        slice_send[slot, 2] = tile
        slice_recv[slot, section] = slice_send[slot]
        for k in range(1, SLICES):
            remote(
                slice_send.at[slot], slice_recv.at[slot, section], xs.at[slot], xr.at[slot], peer(MEMBERS * k), mx
            ).start()

    def slice_wait(slot, sending):
        part = pl.ds(0, SLICES - 1)
        return remote(slice_recv.at[slot, part], slice_recv.at[slot, part], xs.at[slot], xr.at[slot], peer(MEMBERS), mx)

    def far_ring(slot):
        slice_wait(slot, False).wait_recv()
        spread = [jnp.broadcast_to(slice_recv[slot, :, 2, i : i + 1, :], (SLICES, 8, 128)) for i in range(3)]
        levels, final = ring_coefficients(*spread, FAR_STEPS, far_prev, far_ahead)
        value = ring_solve(slice_recv[slot, :, 0], slice_recv[slot, :, 1], levels, final, FAR_STEPS, far_prev, far_ahead)
        ring_values[slot, 0] = value
        ring_values[slot, 1] = far_ahead(value, 1)
        following = ring_values[slot, 1, section]
        solved = expand_block(
            ring_values[slot, 0, section], following, MEMBERS, coefficient_load(4 + slot), odd_load(FAR + 1 + slot)
        )
        sep_send[slot, :, 0] = solved
        sep_send[slot, :, 1] = jnp.concatenate([solved[1:], following[None]], axis=0)
        sep_recv[MEMBERS * slot + member] = sep_send[slot, member]
        for k in range(1, MEMBERS):
            remote(
                sep_send.at[slot, mate(k)], sep_recv.at[MEMBERS * slot + member], ss.at[slot], sr.at[slot],
                MEMBERS * section + mate(k), mx,
            ).start()

    def sep_wait(slot, count):
        return remote(
            sep_send.at[slot, pl.ds(0, count)], sep_recv.at[pl.ds(0, count)], ss.at[slot], sr.at[slot],
            MEMBERS * section + mate(1), mx,
        )

    def each_slot(step):
        @functools.partial(each, SLOTS)
        def _(slot):
            pl.when(MEMBERS * slot + member < FAR)(lambda: step(slot))

    def send_back(f):
        @functools.partial(each, others)
        def _(i):
            k = peer(offset(i))
            remote(back_send.at[f, k], back_recv.at[f, me], bs.at[f], br.at[f], k, mx).start()

    def back_wait(f):
        whole = pl.ds(0, others)
        return remote(back_send.at[f, whole], back_recv.at[f, whole], bs.at[f], br.at[f], peer(1), mx)

    def lay_rows(points, sign):
        total, difference = points[:4] + points[4:], points[:4] - points[4:]
        total = jnp.concatenate([total[m] for m in range(4)], axis=1)
        difference = jnp.concatenate([difference[m] for m in range(4)], axis=1)
        rows_ref[0, 0:64] = total
        rows_ref[0, 64:128] = total
        rows_ref[1, 0:64] = difference
        rows_ref[1, 64:128] = sign * difference

    def kernel_rows():
        links_wait.wait_recv()
        for copy in const_loads:
            copy.wait()
        for odd in range(2):
            dft_v[2 * odd], dft_v[2 * odd + 1] = split(dft_raw[odd])
        idft_v[0], idft_v[1] = split(idft_raw[...])
        pieces = links_recv[...].reshape(8, 2, 8, 128)
        lags = jnp.where(lane[None] < 64, swap_halves(pieces[:, 0].reshape(64, 128)).reshape(8, 8, 128), pieces[:, 1])
        lay_rows(jnp.concatenate([lags] * 8, axis=1), 1.0)

    def kernel_spectrum():
        first_row = lax.broadcasted_iota(jnp.int32, (256, 128), 0) == 0
        real, imag = freq_ref[0, 0:256], freq_ref[0, 256:512]
        spectrum[0] = real
        spectrum[1] = jnp.where(first_row, 0.0, imag)
        spectrum[2] = jnp.where(first_row, imag, real)
        spectrum[3] = freq_ref[1, 0:256]
        spectrum[4] = freq_ref[1, 256:512]

    def near_coefficients():
        @functools.partial(each, 8)
        def _(s):
            rows = jnp.concatenate([links_recv[s]] * 8 + [links_recv[8 + s]] * 8, axis=0)
            link_rows[pl.ds(s, NB, stride=8), :] = rows.T[:NB]

        reduced = coefficients(link_rows[...].reshape(NB, 8, 128), unit, None, coefficient_store(0))
        levels, final = ring_coefficients(*reduced, NEAR_STEPS, near_prev, near_ahead)
        for index, (alpha, beta) in enumerate(levels):
            ring_ref[2 * index] = alpha
            ring_ref[2 * index + 1] = beta
        ring_ref[8] = final

    def near_rows(f):
        near_wait(f).wait_recv()
        pieces = near_recv[f].reshape(8, 2, 4, 8, 128)
        low, high = pieces[:, 0].reshape(256, 128), pieces[:, 1].reshape(256, 128)
        left = lax.broadcasted_iota(jnp.int32, (256, 128), 1) < 64
        plane_a = jnp.where(left, low, swap_halves(high)).reshape(8, 4, 8, 128)
        plane_b = jnp.where(left, swap_halves(low), high).reshape(8, 4, 8, 128)
        lay_rows(jnp.stack([plane_a, plane_b], axis=2).reshape(8, 64, 128), -1.0)

    def near_solve(f):
        real, imag = freq_ref[0, 0:256], freq_ref[0, 256:512]
        odd_real, odd_imag = freq_ref[1, 0:256], freq_ref[1, 256:512]
        product = jnp.concatenate(
            [
                real * spectrum[0] - imag * spectrum[1],
                real * spectrum[1] + imag * spectrum[2],
                odd_real * spectrum[3] - odd_imag * spectrum[4],
                odd_real * spectrum[4] + odd_imag * spectrum[3],
            ],
            axis=0,
        )
        filtered = inverse_transform(idft_v, product).reshape(NB, 8, 128)
        first, onward = reduce_block(filtered, None, coefficient_load(0), odd_keep(FAR))
        ring = [(ring_ref[2 * i], ring_ref[2 * i + 1]) for i in range(4)]
        first = ring_solve(first, onward, ring, ring_ref[8], NEAR_STEPS, near_prev, near_ahead)
        solved = expand_block(first, near_ahead(first, 1), NB, coefficient_load(0), odd_load(FAR))
        work[...] = solved.reshape(512, 128)

        @functools.partial(each, 8)
        def _(s):
            part = work[pl.ds(s, NB, stride=8), :]
            tiles = jnp.concatenate([part, pltpu.roll(part, 120, 1)], axis=0).T
            tiles = tiles.reshape(2, 4, 2, 8, 128)[:, :, 0]
            back_send[f, s] = tiles[0]
            back_send[f, 8 + s] = tiles[1]

        back_recv[f, me] = back_send[f, me]
        send_back(f)

    @functools.partial(each, NF + 1)
    def _(step):
        pl.when(step == 0)(kernel_rows)
        pl.when(step > 0)(lambda: near_rows(step - 1))

        @functools.partial(each, 2)
        def _(odd):
            freq_ref[odd] = forward_transform(dft_v, odd, rows_ref[odd])

        @pl.when(step == 0)
        def _():
            kernel_spectrum()
            near_coefficients()

        pl.when(step > 0)(lambda: near_solve(step - 1))
        pl.when(step == 1)(lambda: each_slot(far_section))
        pl.when(step == 2)(lambda: each_slot(far_ring))

    for slot in range(2):
        sep_wait(slot, MEMBERS - 1).wait_recv()
    pl.when(member != 0)(lambda: sep_wait(2, 1).wait_recv())

    @functools.partial(each, FAR)
    def _(w):
        f, lt = w // FAR_TILES, lax.rem(w, FAR_TILES)
        lanes = pl.ds(pl.multiple_of(128 * lt + NEAR, 128), 128)
        solved = expand_block(sep_recv[w, 0], sep_recv[w, 1], NB, coefficient_load(lt + 1), odd_load(w))
        for j in range(NB):
            work[pl.ds(j, 8, stride=NB), :] = solved[j]
        out[f, :, lanes] = work[...]

    kernel_wait.wait_send()
    links_wait.wait_send()
    each(NF, lambda f: near_wait(f).wait_send())
    for slot in range(2):
        far_wait(slot, MEMBERS - 1).wait_send()
    pl.when(member != 0)(lambda: far_wait(2, 1).wait_send())

    @each_slot
    def _(slot):
        slice_wait(slot, True).wait_send()
        sep_wait(slot, MEMBERS - 1).wait_send()

    @functools.partial(each, NF)
    def _(f):
        back_wait(f).wait_recv()

        @functools.partial(each, 4)
        def _(k):
            tile = back_recv[f, :, k].reshape(128, 128).T
            out[f, pl.ds(pl.multiple_of(128 * k, 128), 128), 0:NEAR] = tile

    each(NF, lambda f: back_wait(f).wait_send())


def body(fields, conduct, kernel):
    dft, idft = transforms()
    shape = fields.shape
    flat = fields.reshape(NF, NX * NB, shape[3])
    vmem = pltpu.VMEM
    dma = pltpu.SemaphoreType.DMA
    anywhere = pl.BlockSpec(memory_space=pl.ANY)
    inside = pl.BlockSpec(memory_space=pltpu.VMEM)
    ax_count = lax.axis_size("ax")
    out = pl.pallas_call(
        kernel_body,
        out_shape=vmem(flat.shape, F32),
        in_specs=[anywhere] * 5,
        out_specs=inside,
        scratch_shapes=[
            vmem((12, 512, 128), F32),
            vmem(conduct.shape, F32),
            vmem(kernel.shape, F32),
            vmem((2, 512, 512), F32),
            vmem((512, 1024), F32),
            vmem((4, 512, 512), BF16),
            vmem((2, 512, 1024), BF16),
            vmem((NF, NQ, 4, 8, 128), F32),
            vmem((NF, NQ, 4, 8, 128), F32),
            vmem((NF, NQ, 4, 8, 128), F32),
            vmem((NF, NQ, 4, 8, 128), F32),
            vmem((ax_count, 8, 128), F32),
            vmem((NQ, 8, 128), F32),
            vmem((NQ, 8, 128), F32),
            vmem((512, 128), F32),
            vmem((2, 128, 512), F32),
            vmem((2, 512, 128), F32),
            vmem((5, 256, 128), F32),
            vmem((4 + SLOTS, NB, 8, 128), F32),
            vmem((4 + SLOTS, NB, 8, 128), F32),
            vmem((4 + SLOTS, NB, 8, 128), F32),
            vmem((9, 8, 128), F32),
            vmem((FAR + 1 + SLOTS, NB, 8, 128), F32),
            vmem((512, 128), F32),
            vmem((FAR, 3, 8, 128), F32),
            vmem((SLOTS, MEMBERS, 3, 8, 128), F32),
            vmem((SLOTS, 3, 8, 128), F32),
            vmem((SLOTS, SLICES, 3, 8, 128), F32),
            vmem((SLOTS, 2, SLICES, 8, 128), F32),
            vmem((SLOTS, MEMBERS, 2, 8, 128), F32),
            vmem((FAR, 2, 8, 128), F32),
            dma((12,)), dma((4,)),
            dma((NF,)), dma((NF,)), dma((NF,)), dma((NF,)),
            dma, dma, dma, dma,
            dma((SLOTS,)), dma((SLOTS,)), dma((SLOTS,)), dma((SLOTS,)), dma((SLOTS,)), dma((SLOTS,)),
        ],
        compiler_params=pltpu.CompilerParams(
            collective_id=0, has_side_effects=True, vmem_limit_bytes=int(60.9 * 2**20)
        ),
    )(flat, conduct, kernel, jnp.asarray(dft), jnp.asarray(idft))
    return out.reshape(shape)


def solution(mesh):
    return jax.shard_map(
        body,
        mesh=mesh,
        in_specs=(P(None, "ax", "az", None), P("az", None), P("ax", "az")),
        out_specs=P(None, "ax", "az", None),
        check_vma=False,
    )
```

```python
import functools

import jax
import jax.numpy as jnp
import numpy as np
from jax import lax
from jax.experimental import pallas as pl
from jax.experimental.pallas import tpu as pltpu
from jax.sharding import PartitionSpec as P

MESH = pl.DeviceIdType.MESH
F32 = jnp.float32
BF16 = jnp.bfloat16

NF = 3
NX = 8
NB = 64
NQ = 16
HALF = NB * NQ // 2
NEAR = 128
FAR_TILES = 3
FAR = NF * FAR_TILES
MEMBERS = 4
SLICES = NQ // MEMBERS
SLOTS = 3
NEAR_STEPS = (1, 2, 4, 8)
FAR_STEPS = (1, 2)
ORDER = (8, 4, 12, 1, 9, 5, 13, 2, 10, 6, 14, 3, 11, 7, 15)


def transforms():
    points = 2 * HALF
    j = np.arange(HALF)
    forward, inverse = [], []
    for odd in (0, 1):
        freq = 2 * np.arange(HALF // 2) + odd
        angle = 2.0 * np.pi * ((freq[:, None] * j[None, :]) % points) / points
        real, imag = np.cos(angle), -np.sin(angle)
        scale = np.full((HALF // 2, 1), 2.0 / points)
        real_back, imag_back = real * scale, imag * scale
        if not odd:
            imag[0] = np.cos(np.pi * j)
            real_back[0] = 1.0 / points
            imag_back[0] = imag[0] / points
        forward.append(np.concatenate([real, imag]))
        inverse.append(np.concatenate([real_back, imag_back]))
    order = (NB * np.arange(8)[None, :] + np.arange(NB)[:, None]).reshape(-1)
    back = np.concatenate(inverse, axis=0).T[order]
    return np.stack(forward).astype(np.float32), back.astype(np.float32)


def split(x):
    high = x.astype(BF16)
    return high, (x - high.astype(F32)).astype(BF16)


def forward_transform(dft_ref, which, rows):
    high, low = split(rows)
    both = jnp.concatenate([high, low], axis=0)
    contract = (((1,), (1,)), ((), ()))
    one = lax.dot_general(dft_ref[2 * which], both, contract, preferred_element_type=F32)
    two = lax.dot_general(dft_ref[2 * which + 1], high, contract, preferred_element_type=F32)
    return one[:, :128] + one[:, 128:] + two


def inverse_transform(idft_ref, spectrum):
    high, low = split(spectrum)
    both = jnp.concatenate([high, low], axis=1)
    contract = (((1,), (0,)), ((), ()))
    one = lax.dot_general(idft_ref[0], both, contract, preferred_element_type=F32)
    two = lax.dot_general(idft_ref[1], high, contract, preferred_element_type=F32)
    return one[:, :128] + one[:, 128:] + two


def place(count):
    return NB - 2 * count


def coefficients(links, excess, onward, store):
    while links.shape[0] > 1:
        count = links.shape[0] // 2
        pairs = links.reshape(count, 2, 8, 128)
        behind, ahead = pairs[:, 0], pairs[:, 1]
        own = excess.reshape(count, 2, 8, 128)
        inv = 1.0 / (behind + ahead + own[:, 1])
        alpha, beta = behind * inv, ahead * inv
        store(place(count), alpha, beta, inv)
        to_left, to_right = alpha * own[:, 1], beta * own[:, 1]
        excess = own[:, 0] + to_left
        if count > 1:
            excess = jnp.concatenate([excess[:1], excess[1:] + to_right[:-1]], axis=0)
        onward = to_right[count - 1] if onward is None else onward + to_right[count - 1]
        links = behind * beta
    return links[0], excess[0], onward


def reduce_block(values, onward, load, keep):
    while values.shape[0] > 1:
        count = values.shape[0] // 2
        pairs = values.reshape(count, 2, 8, 128)
        even, odd = pairs[:, 0], pairs[:, 1]
        keep(place(count), odd)
        alpha, beta, _ = load(place(count), count)
        to_right = beta * odd
        values = even + alpha * odd
        if count > 1:
            values = jnp.concatenate([values[:1], values[1:] + to_right[:-1]], axis=0)
        onward = to_right[count - 1] if onward is None else onward + to_right[count - 1]
    return values[0], onward


def expand_block(first, following, length, load, kept):
    solved = first[None]
    while solved.shape[0] < length:
        count = solved.shape[0]
        alpha, beta, inv = load(place(count), count)
        right = following[None]
        if count > 1:
            right = jnp.concatenate([solved[1:], right], axis=0)
        odd = inv * kept(place(count), count) + alpha * solved + beta * right
        solved = jnp.stack([solved, odd], axis=1).reshape(2 * count, 8, 128)
    return solved


def ring_coefficients(link, first, onward, steps, prev, ahead):
    excess = first + prev(onward, 1)
    after, before = link, prev(link, 1)
    levels = []
    for d in steps:
        inv = 1.0 / (excess + before + after)
        alpha, beta = before * prev(inv, d), after * ahead(inv, d)
        levels.append((alpha, beta))
        excess = excess + alpha * prev(excess, d) + beta * ahead(excess, d)
        if d < steps[-1]:
            before, after = alpha * prev(before, d), beta * ahead(after, d)
    return levels, 1.0 / excess


def ring_solve(first, onward, levels, final, steps, prev, ahead):
    value = first + prev(onward, 1)
    for d, (alpha, beta) in zip(steps, levels):
        value = value + alpha * prev(value, d) + beta * ahead(value, d)
    return value * final


def far_prev(v, d):
    return jnp.concatenate([v[-d:], v[:-d]], axis=0)


def far_ahead(v, d):
    return jnp.concatenate([v[d:], v[:d]], axis=0)


def twin(v):
    return jnp.stack([v, pltpu.roll(v, 64, 1)])


def near_shift(v, d, ahead):
    if d == 8:
        return jnp.stack([v[1], v[0]])
    row = lax.broadcasted_iota(jnp.int32, (8, 128), 0)
    inside = row < 8 - d if ahead else row >= d
    turn = 8 - d if ahead else d
    one, two = pltpu.roll(v[0], turn, 0), pltpu.roll(v[1], turn, 0)
    return jnp.stack([jnp.where(inside, one, two), jnp.where(inside, two, one)])


def near_prev(v, d):
    return near_shift(v, d, False)


def near_ahead(v, d):
    return near_shift(v, d, True)


def swap_halves(x):
    return pltpu.roll(x, 64, x.ndim - 1)


def each(count, step):
    def run(i, carry):
        step(i)
        return carry

    lax.fori_loop(0, count, run, 0)


def wrap(i, count):
    return jnp.where(i >= count, i - count, i)


def kernel_body(
    fields, conduct_hbm, kernel_hbm, dft, idft, out,
    held, conduct, kernel, dft_raw, idft_raw, dft_v, idft_v, near_send, near_recv, back_send, back_recv,
    kernel_all, links_send, links_recv, link_rows, rows_ref, freq_ref, spectrum,
    alpha_ref, beta_ref, inv_ref, ring_ref, odd_ref, work,
    far_send, far_recv, slice_send, slice_recv, ring_values, sep_send, sep_recv,
    load_sem, const_sem, ns, nr, bs, br, ks, kr, cs, cr, fs, fr, xs, xr, ss, sr,
):
    me = lax.axis_index("az")
    mx = lax.axis_index("ax")
    ax_count = lax.axis_size("ax")
    member, section = lax.rem(me, MEMBERS), me // MEMBERS
    others = NQ - 1

    def peer(k):
        return wrap(me + k, NQ)

    def plane(k):
        return wrap(mx + k, ax_count)

    def mate(k):
        return wrap(member + k, MEMBERS)

    def remote(src, dst, send, recv, az, ax):
        return pltpu.make_async_remote_copy(
            src, dst, send, recv, device_id={"az": az, "ax": ax}, device_id_type=MESH
        )

    barrier = pltpu.get_barrier_semaphore()

    for k in ORDER:
        pl.semaphore_signal(barrier, inc=1, device_id={"az": peer(k), "ax": mx}, device_id_type=MESH)
    for k in range(1, ax_count):
        pl.semaphore_signal(barrier, inc=1, device_id={"az": me, "ax": plane(k)}, device_id_type=MESH)

    def load(f, tile):
        return pltpu.make_async_copy(
            fields.at[f, :, pl.ds(pl.multiple_of(128 * tile, 128), 128)], held.at[f * 4 + tile], load_sem.at[f * 4 + tile]
        )

    small_loads = [
        pltpu.make_async_copy(kernel_hbm, kernel, const_sem.at[2]),
        pltpu.make_async_copy(conduct_hbm, conduct, const_sem.at[3]),
    ]
    const_loads = [
        pltpu.make_async_copy(dft, dft_raw, const_sem.at[0]),
        pltpu.make_async_copy(idft, idft_raw, const_sem.at[1]),
    ]
    each(NF, lambda f: load(f, 0).start())
    for copy in small_loads:
        copy.start()
    each(NF, lambda f: each(FAR_TILES, lambda lt: load(f, lt + 1).start()))
    for copy in const_loads:
        copy.start()

    def transpose_near(f):
        load(f, 0).wait()

        @functools.partial(each, 4)
        def _(k):
            part = held[f * 4, pl.ds(pl.multiple_of(128 * k, 128), 128), :]
            near_send[f, :, k] = part.T.reshape(NQ, 8, 128)

        near_recv[f, me] = near_send[f, me]

    transpose_near(0)
    for copy in small_loads:
        copy.wait()
    kernel_all[mx] = jnp.concatenate([kernel[0:8, :], kernel[8:16, :]], axis=1)

    pl.semaphore_wait(barrier, others + ax_count - 1)


    kernel_whole = kernel_all.at[pl.ds(0, ax_count - 1)]
    kernel_wait = remote(kernel_whole, kernel_whole, ks, kr, me, plane(1))

    def send_near(f):
        for k in map(peer, ORDER):
            remote(near_send.at[f, k], near_recv.at[f, me], ns.at[f], nr.at[f], k, mx).start()

    def near_wait(f):
        whole = pl.ds(0, others)
        return remote(near_send.at[f, whole], near_recv.at[f, whole], ns.at[f], nr.at[f], peer(1), mx)

    send_near(0)
    for k in range(1, ax_count):
        remote(kernel_all.at[mx], kernel_all.at[mx], ks, kr, me, plane(k)).start()
    transpose_near(1)
    transpose_near(2)
    row = lax.broadcasted_iota(jnp.int32, (8, 128), 0)
    lane = lax.broadcasted_iota(jnp.int32, (8, 128), 1)

    def coefficient_store(c):
        def store(offset, alpha, beta, inv):
            count = alpha.shape[0]
            alpha_ref[c, offset : offset + count] = alpha
            beta_ref[c, offset : offset + count] = beta
            inv_ref[c, offset : offset + count] = inv

        return store

    def coefficient_load(c):
        def load(offset, count):
            return (
                alpha_ref[c, offset : offset + count],
                beta_ref[c, offset : offset + count],
                inv_ref[c, offset : offset + count],
            )

        return load

    def odd_keep(w):
        def keep(offset, value):
            odd_ref[w, offset : offset + value.shape[0]] = value

        return keep

    def odd_load(w):
        return lambda offset, count: odd_ref[w, offset : offset + count]

    unit = jnp.ones((NB, 8, 128), F32)

    def packed(link, first, onward):
        return jnp.where(row == 0, link, jnp.where(row == 1, first, onward))

    @functools.partial(each, FAR_TILES)
    def _(lt):
        lanes = pl.ds(pl.multiple_of(128 * lt + NEAR, 128), 128)
        links = jnp.stack([jnp.broadcast_to(conduct[j : j + 1, lanes], (8, 128)) for j in range(NB)])
        tile = packed(*coefficients(links, unit, None, coefficient_store(lt + 1)))
        for f in range(NF):
            far_send[f * FAR_TILES + lt, 2] = tile

    each(NF, lambda f: each(FAR_TILES, lambda lt: load(f, lt + 1).wait()))

    def far_reduce(f, lt):
        w = f * FAR_TILES + lt
        values = jnp.stack([held[f * 4 + lt + 1, pl.ds(j, 8, stride=NB), :] for j in range(NB)])
        first, onward = reduce_block(values, None, coefficient_load(lt + 1), odd_keep(w))
        far_send[w, 0] = first
        far_send[w, 1] = onward

    each(NF, lambda f: each(FAR_TILES, lambda lt: far_reduce(f, lt)))

    for w in range(FAR):
        slot, owner = w // MEMBERS, w % MEMBERS

        @pl.when(member == owner)
        def _():
            far_recv[slot, member] = far_send[w]

        @pl.when(member != owner)
        def _():
            remote(
                far_send.at[w], far_recv.at[slot, member], fs.at[slot], fr.at[slot], MEMBERS * section + owner, mx
            ).start()

    def far_wait(slot, count):
        return remote(
            far_send.at[pl.ds(0, count)], far_recv.at[slot, pl.ds(0, count)], fs.at[slot], fr.at[slot],
            MEMBERS * section + mate(1), mx,
        )

    near_links = conduct[:, :NEAR]
    near_links = jnp.concatenate([near_links, near_links], axis=0).T.reshape(NQ, 8, 128)
    kernel_wait.wait_recv()
    kernels = kernel_all[...]
    swapped = swap_halves(kernels.reshape(64, 128)).reshape(8, 8, 128)
    kernels = jnp.stack([swapped, kernels], axis=1).reshape(NQ, 8, 128)
    links_send[...] = jnp.where(lane[None] < 64, near_links, kernels)
    links_recv[me] = links_send[me]

    for k in map(peer, ORDER):
        remote(links_send.at[k], links_recv.at[me], cs, cr, k, mx).start()

    links_wait = remote(links_send.at[pl.ds(0, others)], links_recv.at[pl.ds(0, others)], cs, cr, peer(1), mx)
    near_wait(0).wait_send()
    send_near(1)

    for copy in const_loads:
        copy.wait()
    for odd in range(2):
        dft_v[2 * odd], dft_v[2 * odd + 1] = split(dft_raw[odd])
    idft_v[0], idft_v[1] = split(idft_raw[...])

    near_wait(1).wait_send()
    send_near(2)

    def far_section(slot):
        far_wait(slot, MEMBERS - 1).wait_recv()
        shape = (MEMBERS, 8, 128)
        link, first, onward = [jnp.broadcast_to(far_recv[slot, :, 2, i : i + 1, :], shape) for i in range(3)]
        first = jnp.concatenate([first[:1], first[1:] + onward[:-1]], axis=0)
        tile = packed(*coefficients(link, first, onward[MEMBERS - 1], coefficient_store(4 + slot)))
        values, onward = far_recv[slot, :, 0], far_recv[slot, :, 1]
        values = jnp.concatenate([values[:1], values[1:] + onward[:-1]], axis=0)
        value, onward = reduce_block(values, onward[MEMBERS - 1], coefficient_load(4 + slot), odd_keep(FAR + 1 + slot))
        slice_send[slot, 0] = value
        slice_send[slot, 1] = onward
        slice_send[slot, 2] = tile
        slice_recv[slot, section] = slice_send[slot]
        for k in range(1, SLICES):
            remote(
                slice_send.at[slot], slice_recv.at[slot, section], xs.at[slot], xr.at[slot], peer(MEMBERS * k), mx
            ).start()

    def slice_wait(slot, sending):
        part = pl.ds(0, SLICES - 1)
        return remote(slice_recv.at[slot, part], slice_recv.at[slot, part], xs.at[slot], xr.at[slot], peer(MEMBERS), mx)

    def far_ring(slot):
        slice_wait(slot, False).wait_recv()
        spread = [jnp.broadcast_to(slice_recv[slot, :, 2, i : i + 1, :], (SLICES, 8, 128)) for i in range(3)]
        levels, final = ring_coefficients(*spread, FAR_STEPS, far_prev, far_ahead)
        value = ring_solve(slice_recv[slot, :, 0], slice_recv[slot, :, 1], levels, final, FAR_STEPS, far_prev, far_ahead)
        ring_values[slot, 0] = value
        ring_values[slot, 1] = far_ahead(value, 1)
        following = ring_values[slot, 1, section]
        solved = expand_block(
            ring_values[slot, 0, section], following, MEMBERS, coefficient_load(4 + slot), odd_load(FAR + 1 + slot)
        )
        sep_send[slot, :, 0] = solved
        sep_send[slot, :, 1] = jnp.concatenate([solved[1:], following[None]], axis=0)
        sep_recv[MEMBERS * slot + member] = sep_send[slot, member]
        for k in range(1, MEMBERS):
            remote(
                sep_send.at[slot, mate(k)], sep_recv.at[MEMBERS * slot + member], ss.at[slot], sr.at[slot],
                MEMBERS * section + mate(k), mx,
            ).start()

    def sep_wait(slot, count):
        return remote(
            sep_send.at[slot, pl.ds(0, count)], sep_recv.at[pl.ds(0, count)], ss.at[slot], sr.at[slot],
            MEMBERS * section + mate(1), mx,
        )

    def each_slot(step):
        @functools.partial(each, SLOTS)
        def _(slot):
            pl.when(MEMBERS * slot + member < FAR)(lambda: step(slot))

    def send_back(f):
        for k in map(peer, ORDER):
            remote(back_send.at[f, k], back_recv.at[f, me], bs.at[f], br.at[f], k, mx).start()

    def back_wait(f):
        whole = pl.ds(0, others)
        return remote(back_send.at[f, whole], back_recv.at[f, whole], bs.at[f], br.at[f], peer(1), mx)

    def lay_rows(points, place):
        total, difference = points[:4] + points[4:], points[:4] - points[4:]
        rows_ref[0, place : place + 64] = jnp.concatenate([total[m] for m in range(4)], axis=1)
        rows_ref[1, place : place + 64] = jnp.concatenate([difference[m] for m in range(4)], axis=1)

    def kernel_rows():
        pieces = links_recv[...].reshape(8, 2, 8, 128)
        lags = jnp.where(lane[None] < 64, swap_halves(pieces[:, 0].reshape(64, 128)).reshape(8, 8, 128), pieces[:, 1])
        lay_rows(jnp.concatenate([lags] * 8, axis=1), 64)

    left = lax.broadcasted_iota(jnp.int32, (256, 128), 1) < 64

    def kernel_spectrum():
        def both(odd, half):
            value = freq_ref[odd, 256 * half : 256 * half + 256]
            return jnp.where(left, swap_halves(value), value)

        first_row = lax.broadcasted_iota(jnp.int32, (256, 128), 0) == 0
        real, imag = both(0, 0), both(0, 1)
        spectrum[0] = real
        spectrum[1] = jnp.where(first_row, 0.0, imag)
        spectrum[2] = jnp.where(first_row, imag, real)
        spectrum[3] = both(1, 0)
        spectrum[4] = both(1, 1)

    def near_coefficients():
        @functools.partial(each, 8)
        def _(s):
            rows = jnp.concatenate([links_recv[s]] * 8 + [links_recv[8 + s]] * 8, axis=0)
            link_rows[pl.ds(s, NB, stride=8), :] = rows.T[:NB]

        reduced = coefficients(link_rows[...].reshape(NB, 8, 128), unit, None, coefficient_store(0))
        levels, final = ring_coefficients(*[twin(v) for v in reduced], NEAR_STEPS, near_prev, near_ahead)
        for index, (alpha, beta) in enumerate(levels):
            ring_ref[2 * index] = alpha
            ring_ref[2 * index + 1] = beta
        ring_ref[8] = final

    def near_rows(f):
        near_wait(f).wait_recv()
        pieces = near_recv[f].reshape(8, 2, 4, 8, 128)
        low, high = pieces[:, 0].reshape(256, 128), pieces[:, 1].reshape(256, 128)
        plane_a = jnp.where(left, low, swap_halves(high)).reshape(8, 4, 8, 128)
        plane_b = jnp.where(left, swap_halves(low), high).reshape(8, 4, 8, 128)
        lay_rows(jnp.stack([plane_a, plane_b], axis=2).reshape(8, 64, 128), 0)

    def near_solve(f):
        def both(odd, half, sign):
            value = freq_ref[odd, 256 * half : 256 * half + 256]
            return jnp.where(left, value, sign * swap_halves(value))

        real, imag = both(0, 0, 1.0), both(0, 1, 1.0)
        odd_real, odd_imag = both(1, 0, -1.0), both(1, 1, -1.0)
        product = jnp.concatenate(
            [
                real * spectrum[0] - imag * spectrum[1],
                real * spectrum[1] + imag * spectrum[2],
                odd_real * spectrum[3] - odd_imag * spectrum[4],
                odd_real * spectrum[4] + odd_imag * spectrum[3],
            ],
            axis=0,
        )
        filtered = inverse_transform(idft_v, product).reshape(NB, 8, 128)
        first, onward = reduce_block(filtered, None, coefficient_load(0), odd_keep(FAR))
        ring = [(ring_ref[2 * i], ring_ref[2 * i + 1]) for i in range(4)]
        first = ring_solve(twin(first), twin(onward), ring, ring_ref[8], NEAR_STEPS, near_prev, near_ahead)
        solved = expand_block(first[0], near_ahead(first, 1)[0], NB, coefficient_load(0), odd_load(FAR))
        work[...] = solved.reshape(512, 128)

        @functools.partial(each, 8)
        def _(s):
            part = work[pl.ds(s, NB, stride=8), :]
            tiles = jnp.concatenate([part, pltpu.roll(part, 120, 1)], axis=0).T
            tiles = tiles.reshape(2, 4, 2, 8, 128)[:, :, 0]
            back_send[f, s] = tiles[0]
            back_send[f, 8 + s] = tiles[1]

        back_recv[f, me] = back_send[f, me]
        send_back(f)

    links_wait.wait_recv()
    kernel_rows()
    near_coefficients()
    each_slot(far_section)

    @functools.partial(each, NF)
    def _(f):
        near_rows(f)

        @functools.partial(each, 2)
        def _(odd):
            freq_ref[odd] = forward_transform(dft_v, odd, rows_ref[odd])

        pl.when(f == 0)(kernel_spectrum)
        near_solve(f)
        pl.when(f == 1)(lambda: each_slot(far_ring))

    for slot in range(2):
        sep_wait(slot, MEMBERS - 1).wait_recv()
    pl.when(member != 0)(lambda: sep_wait(2, 1).wait_recv())

    def far_expand(f, lt):
        w = f * FAR_TILES + lt
        lanes = pl.ds(pl.multiple_of(128 * lt + NEAR, 128), 128)
        solved = expand_block(sep_recv[w, 0], sep_recv[w, 1], NB, coefficient_load(lt + 1), odd_load(w))
        for j in range(NB):
            work[pl.ds(j, 8, stride=NB), :] = solved[j]
        out[f, :, lanes] = work[...]

    each(NF, lambda f: each(FAR_TILES, lambda lt: far_expand(f, lt)))

    kernel_wait.wait_send()
    links_wait.wait_send()
    near_wait(2).wait_send()
    for slot in range(2):
        far_wait(slot, MEMBERS - 1).wait_send()
    pl.when(member != 0)(lambda: far_wait(2, 1).wait_send())

    @each_slot
    def _(slot):
        slice_wait(slot, True).wait_send()
        sep_wait(slot, MEMBERS - 1).wait_send()

    @functools.partial(each, NF)
    def _(f):
        back_wait(f).wait_recv()

        @functools.partial(each, 4)
        def _(k):
            tile = back_recv[f, :, k].reshape(128, 128).T
            out[f, pl.ds(pl.multiple_of(128 * k, 128), 128), 0:NEAR] = tile

    each(NF, lambda f: back_wait(f).wait_send())


def body(fields, conduct, kernel):
    dft, idft = transforms()
    shape = fields.shape
    flat = fields.reshape(NF, NX * NB, shape[3])
    vmem = pltpu.VMEM
    dma = pltpu.SemaphoreType.DMA
    anywhere = pl.BlockSpec(memory_space=pl.ANY)
    inside = pl.BlockSpec(memory_space=pltpu.VMEM)
    ax_count = lax.axis_size("ax")
    out = pl.pallas_call(
        kernel_body,
        out_shape=vmem(flat.shape, F32),
        in_specs=[anywhere] * 5,
        out_specs=inside,
        scratch_shapes=[
            vmem((12, 512, 128), F32),
            vmem(conduct.shape, F32),
            vmem(kernel.shape, F32),
            vmem((2, 512, 512), F32),
            vmem((512, 1024), F32),
            vmem((4, 512, 512), BF16),
            vmem((2, 512, 1024), BF16),
            vmem((NF, NQ, 4, 8, 128), F32),
            vmem((NF, NQ, 4, 8, 128), F32),
            vmem((NF, NQ, 4, 8, 128), F32),
            vmem((NF, NQ, 4, 8, 128), F32),
            vmem((ax_count, 8, 128), F32),
            vmem((NQ, 8, 128), F32),
            vmem((NQ, 8, 128), F32),
            vmem((512, 128), F32),
            vmem((2, 128, 512), F32),
            vmem((2, 512, 128), F32),
            vmem((5, 256, 128), F32),
            vmem((4 + SLOTS, NB, 8, 128), F32),
            vmem((4 + SLOTS, NB, 8, 128), F32),
            vmem((4 + SLOTS, NB, 8, 128), F32),
            vmem((9, 2, 8, 128), F32),
            vmem((FAR + 1 + SLOTS, NB, 8, 128), F32),
            vmem((512, 128), F32),
            vmem((FAR, 3, 8, 128), F32),
            vmem((SLOTS, MEMBERS, 3, 8, 128), F32),
            vmem((SLOTS, 3, 8, 128), F32),
            vmem((SLOTS, SLICES, 3, 8, 128), F32),
            vmem((SLOTS, 2, SLICES, 8, 128), F32),
            vmem((SLOTS, MEMBERS, 2, 8, 128), F32),
            vmem((FAR, 2, 8, 128), F32),
            dma((12,)), dma((4,)),
            dma((NF,)), dma((NF,)), dma((NF,)), dma((NF,)),
            dma, dma, dma, dma,
            dma((SLOTS,)), dma((SLOTS,)), dma((SLOTS,)), dma((SLOTS,)), dma((SLOTS,)), dma((SLOTS,)),
        ],
        compiler_params=pltpu.CompilerParams(
            collective_id=0, has_side_effects=True, vmem_limit_bytes=int(60.9 * 2**20)
        ),
    )(flat, conduct, kernel, jnp.asarray(dft), jnp.asarray(idft))
    return out.reshape(shape)


def solution(mesh):
    return jax.shard_map(
        body,
        mesh=mesh,
        in_specs=(P(None, "ax", "az", None), P("az", None), P("ax", "az")),
        out_specs=P(None, "ax", "az", None),
        check_vma=False,
    )
```

```python
import functools

import jax
import jax.numpy as jnp
import numpy as np
from jax import lax
from jax.experimental import pallas as pl
from jax.experimental.pallas import tpu as pltpu
from jax.sharding import PartitionSpec as P

MESH = pl.DeviceIdType.MESH
F32 = jnp.float32
BF16 = jnp.bfloat16

NF = 3
NX = 8
NB = 64
NQ = 16
HALF = NB * NQ // 2
NEAR = 128
FAR_TILES = 3
FAR = NF * FAR_TILES
MEMBERS = 4
SLICES = NQ // MEMBERS
SLOTS = 3
NEAR_STEPS = (1, 2, 4, 8)
FAR_STEPS = (1, 2)
ORDER = (8, 4, 12, 1, 9, 5, 13, 2, 10, 6, 14, 3, 11, 7, 15)


def transforms():
    points = 2 * HALF
    j = np.arange(HALF)
    forward, inverse = [], []
    for odd in (0, 1):
        freq = 2 * np.arange(HALF // 2) + odd
        angle = 2.0 * np.pi * ((freq[:, None] * j[None, :]) % points) / points
        real, imag = np.cos(angle), -np.sin(angle)
        scale = np.full((HALF // 2, 1), 2.0 / points)
        real_back, imag_back = real * scale, imag * scale
        if not odd:
            imag[0] = np.cos(np.pi * j)
            real_back[0] = 1.0 / points
            imag_back[0] = imag[0] / points
        forward.append(np.concatenate([real, imag]))
        inverse.append(np.concatenate([real_back, imag_back]))
    order = (NB * np.arange(8)[None, :] + np.arange(NB)[:, None]).reshape(-1)
    back = np.concatenate(inverse, axis=0).T[order]
    return np.stack(forward).astype(np.float32), back.astype(np.float32)


def split(x):
    high = x.astype(BF16)
    return high, (x - high.astype(F32)).astype(BF16)


def forward_transform(dft_ref, which, rows):
    high, low = split(rows)
    both = jnp.concatenate([high, low], axis=0)
    contract = (((1,), (1,)), ((), ()))
    one = lax.dot_general(dft_ref[2 * which], both, contract, preferred_element_type=F32)
    two = lax.dot_general(dft_ref[2 * which + 1], high, contract, preferred_element_type=F32)
    return one[:, :128] + one[:, 128:] + two


def inverse_transform(idft_ref, spectrum):
    high, low = split(spectrum)
    both = jnp.concatenate([high, low], axis=1)
    contract = (((1,), (0,)), ((), ()))
    one = lax.dot_general(idft_ref[0], both, contract, preferred_element_type=F32)
    two = lax.dot_general(idft_ref[1], high, contract, preferred_element_type=F32)
    return one[:, :128] + one[:, 128:] + two


def place(count):
    return NB - 2 * count


def coefficients(links, excess, onward, store):
    while links.shape[0] > 1:
        count = links.shape[0] // 2
        pairs = links.reshape(count, 2, 8, 128)
        behind, ahead = pairs[:, 0], pairs[:, 1]
        own = excess.reshape(count, 2, 8, 128)
        inv = 1.0 / (behind + ahead + own[:, 1])
        alpha, beta = behind * inv, ahead * inv
        store(place(count), alpha, beta, inv)
        to_left, to_right = alpha * own[:, 1], beta * own[:, 1]
        excess = own[:, 0] + to_left
        if count > 1:
            excess = jnp.concatenate([excess[:1], excess[1:] + to_right[:-1]], axis=0)
        onward = to_right[count - 1] if onward is None else onward + to_right[count - 1]
        links = behind * beta
    return links[0], excess[0], onward


def reduce_block(values, onward, load, keep):
    while values.shape[0] > 1:
        count = values.shape[0] // 2
        pairs = values.reshape(count, 2, 8, 128)
        even, odd = pairs[:, 0], pairs[:, 1]
        keep(place(count), odd)
        alpha, beta, _ = load(place(count), count)
        to_right = beta * odd
        values = even + alpha * odd
        if count > 1:
            values = jnp.concatenate([values[:1], values[1:] + to_right[:-1]], axis=0)
        onward = to_right[count - 1] if onward is None else onward + to_right[count - 1]
    return values[0], onward


def expand_block(first, following, length, load, kept):
    solved = first[None]
    while solved.shape[0] < length:
        count = solved.shape[0]
        alpha, beta, inv = load(place(count), count)
        right = following[None]
        if count > 1:
            right = jnp.concatenate([solved[1:], right], axis=0)
        odd = inv * kept(place(count), count) + alpha * solved + beta * right
        solved = jnp.stack([solved, odd], axis=1).reshape(2 * count, 8, 128)
    return solved


def ring_coefficients(link, first, onward, steps, prev, ahead):
    excess = first + prev(onward, 1)
    after, before = link, prev(link, 1)
    levels = []
    for d in steps:
        inv = 1.0 / (excess + before + after)
        alpha, beta = before * prev(inv, d), after * ahead(inv, d)
        levels.append((alpha, beta))
        excess = excess + alpha * prev(excess, d) + beta * ahead(excess, d)
        if d < steps[-1]:
            before, after = alpha * prev(before, d), beta * ahead(after, d)
    return levels, 1.0 / excess


def ring_solve(first, onward, levels, final, steps, prev, ahead):
    value = first + prev(onward, 1)
    for d, (alpha, beta) in zip(steps, levels):
        value = value + alpha * prev(value, d) + beta * ahead(value, d)
    return value * final


def far_prev(v, d):
    return jnp.concatenate([v[-d:], v[:-d]], axis=0)


def far_ahead(v, d):
    return jnp.concatenate([v[d:], v[:d]], axis=0)


def twin(v):
    return jnp.stack([v, pltpu.roll(v, 64, 1)])


def near_shift(v, d, ahead):
    if d == 8:
        return jnp.stack([v[1], v[0]])
    row = lax.broadcasted_iota(jnp.int32, (8, 128), 0)
    inside = row < 8 - d if ahead else row >= d
    turn = 8 - d if ahead else d
    one, two = pltpu.roll(v[0], turn, 0), pltpu.roll(v[1], turn, 0)
    return jnp.stack([jnp.where(inside, one, two), jnp.where(inside, two, one)])


def near_prev(v, d):
    return near_shift(v, d, False)


def near_ahead(v, d):
    return near_shift(v, d, True)


def swap_halves(x):
    return pltpu.roll(x, 64, x.ndim - 1)


def each(count, step):
    def run(i, carry):
        step(i)
        return carry

    lax.fori_loop(0, count, run, 0)


def wrap(i, count):
    return jnp.where(i >= count, i - count, i)


def kernel_body(
    fields, conduct_hbm, kernel_hbm, dft, idft, out,
    held, conduct, kernel, dft_raw, idft_raw, dft_v, idft_v, near_send, near_recv, back_send, back_recv,
    kernel_all, links_send, links_recv, link_rows, rows_ref, freq_ref, spectrum,
    alpha_ref, beta_ref, inv_ref, ring_ref, odd_ref, work,
    far_send, far_recv, slice_send, slice_recv, ring_values, sep_send, sep_recv,
    load_sem, const_sem, ns, nr, bs, br, ks, kr, cs, cr, fs, fr, xs, xr, ss, sr,
):
    me = lax.axis_index("az")
    mx = lax.axis_index("ax")
    ax_count = lax.axis_size("ax")
    member, section = lax.rem(me, MEMBERS), me // MEMBERS
    others = NQ - 1

    def peer(k):
        return wrap(me + k, NQ)

    def plane(k):
        return wrap(mx + k, ax_count)

    def mate(k):
        return wrap(member + k, MEMBERS)

    def remote(src, dst, send, recv, az, ax):
        return pltpu.make_async_remote_copy(
            src, dst, send, recv, device_id={"az": az, "ax": ax}, device_id_type=MESH
        )

    barrier = pltpu.get_barrier_semaphore()

    for k in ORDER:
        pl.semaphore_signal(barrier, inc=1, device_id={"az": peer(k), "ax": mx}, device_id_type=MESH)
    for k in range(1, ax_count):
        pl.semaphore_signal(barrier, inc=1, device_id={"az": me, "ax": plane(k)}, device_id_type=MESH)

    def load(f, tile):
        return pltpu.make_async_copy(
            fields.at[f, :, pl.ds(pl.multiple_of(128 * tile, 128), 128)], held.at[f * 4 + tile], load_sem.at[f * 4 + tile]
        )

    small_loads = [
        pltpu.make_async_copy(kernel_hbm, kernel, const_sem.at[2]),
        pltpu.make_async_copy(conduct_hbm, conduct, const_sem.at[3]),
    ]
    const_loads = [
        pltpu.make_async_copy(dft, dft_raw, const_sem.at[0]),
        pltpu.make_async_copy(idft, idft_raw, const_sem.at[1]),
    ]
    each(NF, lambda f: load(f, 0).start())
    for copy in small_loads:
        copy.start()
    each(NF, lambda f: each(FAR_TILES, lambda lt: load(f, lt + 1).start()))
    for copy in const_loads:
        copy.start()

    def transpose_near(f):
        load(f, 0).wait()

        @functools.partial(each, 4)
        def _(k):
            part = held[f * 4, pl.ds(pl.multiple_of(128 * k, 128), 128), :]
            near_send[f, :, k] = part.T.reshape(NQ, 8, 128)

        near_recv[f, me] = near_send[f, me]

    transpose_near(0)
    for copy in small_loads:
        copy.wait()
    kernel_all[mx] = jnp.concatenate([kernel[0:8, :], kernel[8:16, :]], axis=1)

    pl.semaphore_wait(barrier, others + ax_count - 1)


    kernel_whole = kernel_all.at[pl.ds(0, ax_count - 1)]
    kernel_wait = remote(kernel_whole, kernel_whole, ks, kr, me, plane(1))

    def send_near(f):
        for k in map(peer, ORDER):
            remote(near_send.at[f, k], near_recv.at[f, me], ns.at[f], nr.at[f], k, mx).start()

    def near_wait(f):
        whole = pl.ds(0, others)
        return remote(near_send.at[f, whole], near_recv.at[f, whole], ns.at[f], nr.at[f], peer(1), mx)

    send_near(0)
    for k in range(1, ax_count):
        remote(kernel_all.at[mx], kernel_all.at[mx], ks, kr, me, plane(k)).start()
    transpose_near(1)
    transpose_near(2)
    row = lax.broadcasted_iota(jnp.int32, (8, 128), 0)
    lane = lax.broadcasted_iota(jnp.int32, (8, 128), 1)

    def coefficient_store(c):
        def store(offset, alpha, beta, inv):
            count = alpha.shape[0]
            alpha_ref[c, offset : offset + count] = alpha
            beta_ref[c, offset : offset + count] = beta
            inv_ref[c, offset : offset + count] = inv

        return store

    def coefficient_load(c):
        def load(offset, count):
            return (
                alpha_ref[c, offset : offset + count],
                beta_ref[c, offset : offset + count],
                inv_ref[c, offset : offset + count],
            )

        return load

    def odd_keep(w):
        def keep(offset, value):
            odd_ref[w, offset : offset + value.shape[0]] = value

        return keep

    def odd_load(w):
        return lambda offset, count: odd_ref[w, offset : offset + count]

    unit = jnp.ones((NB, 8, 128), F32)

    def packed(link, first, onward):
        return jnp.where(row == 0, link, jnp.where(row == 1, first, onward))

    @functools.partial(each, FAR_TILES)
    def _(lt):
        lanes = pl.ds(pl.multiple_of(128 * lt + NEAR, 128), 128)
        links = jnp.stack([jnp.broadcast_to(conduct[j : j + 1, lanes], (8, 128)) for j in range(NB)])
        tile = packed(*coefficients(links, unit, None, coefficient_store(lt + 1)))
        for f in range(NF):
            far_send[f * FAR_TILES + lt, 2] = tile

    each(NF, lambda f: each(FAR_TILES, lambda lt: load(f, lt + 1).wait()))

    def far_reduce(f, lt):
        w = f * FAR_TILES + lt
        values = jnp.stack([held[f * 4 + lt + 1, pl.ds(j, 8, stride=NB), :] for j in range(NB)])
        first, onward = reduce_block(values, None, coefficient_load(lt + 1), odd_keep(w))
        far_send[w, 0] = first
        far_send[w, 1] = onward

    each(NF, lambda f: each(FAR_TILES, lambda lt: far_reduce(f, lt)))

    for w in range(FAR):
        slot, owner = w // MEMBERS, w % MEMBERS

        @pl.when(member == owner)
        def _():
            far_recv[slot, member] = far_send[w]

        @pl.when(member != owner)
        def _():
            remote(
                far_send.at[w], far_recv.at[slot, member], fs.at[slot], fr.at[slot], MEMBERS * section + owner, mx
            ).start()

    def far_wait(slot, count):
        return remote(
            far_send.at[pl.ds(0, count)], far_recv.at[slot, pl.ds(0, count)], fs.at[slot], fr.at[slot],
            MEMBERS * section + mate(1), mx,
        )

    near_links = conduct[:, :NEAR]
    near_links = jnp.concatenate([near_links, near_links], axis=0).T.reshape(NQ, 8, 128)
    kernel_wait.wait_recv()
    kernels = kernel_all[...]
    swapped = swap_halves(kernels.reshape(64, 128)).reshape(8, 8, 128)
    kernels = jnp.stack([swapped, kernels], axis=1).reshape(NQ, 8, 128)
    links_send[...] = jnp.where(lane[None] < 64, near_links, kernels)
    links_recv[me] = links_send[me]

    for k in map(peer, ORDER):
        remote(links_send.at[k], links_recv.at[me], cs, cr, k, mx).start()

    links_wait = remote(links_send.at[pl.ds(0, others)], links_recv.at[pl.ds(0, others)], cs, cr, peer(1), mx)
    near_wait(0).wait_send()
    send_near(1)

    for copy in const_loads:
        copy.wait()
    for odd in range(2):
        dft_v[2 * odd], dft_v[2 * odd + 1] = split(dft_raw[odd])
    idft_v[0], idft_v[1] = split(idft_raw[...])

    near_wait(1).wait_send()
    send_near(2)

    def far_section(slot):
        far_wait(slot, MEMBERS - 1).wait_recv()
        shape = (MEMBERS, 8, 128)
        link, first, onward = [jnp.broadcast_to(far_recv[slot, :, 2, i : i + 1, :], shape) for i in range(3)]
        first = jnp.concatenate([first[:1], first[1:] + onward[:-1]], axis=0)
        tile = packed(*coefficients(link, first, onward[MEMBERS - 1], coefficient_store(4 + slot)))
        values, onward = far_recv[slot, :, 0], far_recv[slot, :, 1]
        values = jnp.concatenate([values[:1], values[1:] + onward[:-1]], axis=0)
        value, onward = reduce_block(values, onward[MEMBERS - 1], coefficient_load(4 + slot), odd_keep(FAR + 1 + slot))
        slice_send[slot, 0] = value
        slice_send[slot, 1] = onward
        slice_send[slot, 2] = tile
        slice_recv[slot, section] = slice_send[slot]
        for k in range(1, SLICES):
            remote(
                slice_send.at[slot], slice_recv.at[slot, section], xs.at[slot], xr.at[slot], peer(MEMBERS * k), mx
            ).start()

    def slice_wait(slot, sending):
        part = pl.ds(0, SLICES - 1)
        return remote(slice_recv.at[slot, part], slice_recv.at[slot, part], xs.at[slot], xr.at[slot], peer(MEMBERS), mx)

    def far_ring(slot):
        slice_wait(slot, False).wait_recv()
        spread = [jnp.broadcast_to(slice_recv[slot, :, 2, i : i + 1, :], (SLICES, 8, 128)) for i in range(3)]
        levels, final = ring_coefficients(*spread, FAR_STEPS, far_prev, far_ahead)
        value = ring_solve(slice_recv[slot, :, 0], slice_recv[slot, :, 1], levels, final, FAR_STEPS, far_prev, far_ahead)
        ring_values[slot, 0] = value
        ring_values[slot, 1] = far_ahead(value, 1)
        following = ring_values[slot, 1, section]
        solved = expand_block(
            ring_values[slot, 0, section], following, MEMBERS, coefficient_load(4 + slot), odd_load(FAR + 1 + slot)
        )
        sep_send[slot, :, 0] = solved
        sep_send[slot, :, 1] = jnp.concatenate([solved[1:], following[None]], axis=0)
        sep_recv[MEMBERS * slot + member] = sep_send[slot, member]
        for k in range(1, MEMBERS):
            remote(
                sep_send.at[slot, mate(k)], sep_recv.at[MEMBERS * slot + member], ss.at[slot], sr.at[slot],
                MEMBERS * section + mate(k), mx,
            ).start()

    def sep_wait(slot, count):
        return remote(
            sep_send.at[slot, pl.ds(0, count)], sep_recv.at[pl.ds(0, count)], ss.at[slot], sr.at[slot],
            MEMBERS * section + mate(1), mx,
        )

    def each_slot(step):
        @functools.partial(each, SLOTS)
        def _(slot):
            pl.when(MEMBERS * slot + member < FAR)(lambda: step(slot))

    def send_back(f):
        for k in map(peer, ORDER):
            remote(back_send.at[f, k], back_recv.at[f, me], bs.at[f], br.at[f], k, mx).start()

    def back_wait(f):
        whole = pl.ds(0, others)
        return remote(back_send.at[f, whole], back_recv.at[f, whole], bs.at[f], br.at[f], peer(1), mx)

    def lay_rows(points, place):
        total, difference = points[:4] + points[4:], points[:4] - points[4:]
        rows_ref[0, place : place + 64] = jnp.concatenate([total[m] for m in range(4)], axis=1)
        rows_ref[1, place : place + 64] = jnp.concatenate([difference[m] for m in range(4)], axis=1)

    def kernel_rows():
        pieces = links_recv[...].reshape(8, 2, 8, 128)
        lags = jnp.where(lane[None] < 64, swap_halves(pieces[:, 0].reshape(64, 128)).reshape(8, 8, 128), pieces[:, 1])
        lay_rows(jnp.concatenate([lags] * 8, axis=1), 64)

    left = lax.broadcasted_iota(jnp.int32, (256, 128), 1) < 64

    def kernel_spectrum():
        def both(odd, half):
            value = freq_ref[odd, 256 * half : 256 * half + 256]
            return jnp.where(left, swap_halves(value), value)

        first_row = lax.broadcasted_iota(jnp.int32, (256, 128), 0) == 0
        real, imag = both(0, 0), both(0, 1)
        spectrum[0] = real
        spectrum[1] = jnp.where(first_row, 0.0, imag)
        spectrum[2] = jnp.where(first_row, imag, real)
        spectrum[3] = both(1, 0)
        spectrum[4] = both(1, 1)

    def near_coefficients():
        for s in range(8):
            rows = jnp.concatenate([links_recv[s]] * 8 + [links_recv[8 + s]] * 8, axis=0)
            link_rows[pl.ds(s, NB, stride=8), :] = rows.T[:NB]

        reduced = coefficients(link_rows[...].reshape(NB, 8, 128), unit, None, coefficient_store(0))
        levels, final = ring_coefficients(*[twin(v) for v in reduced], NEAR_STEPS, near_prev, near_ahead)
        for index, (alpha, beta) in enumerate(levels):
            ring_ref[2 * index] = alpha
            ring_ref[2 * index + 1] = beta
        ring_ref[8] = final

    def near_rows(f):
        near_wait(f).wait_recv()
        pieces = near_recv[f].reshape(8, 2, 4, 8, 128)
        low, high = pieces[:, 0].reshape(256, 128), pieces[:, 1].reshape(256, 128)
        plane_a = jnp.where(left, low, swap_halves(high)).reshape(8, 4, 8, 128)
        plane_b = jnp.where(left, swap_halves(low), high).reshape(8, 4, 8, 128)
        lay_rows(jnp.stack([plane_a, plane_b], axis=2).reshape(8, 64, 128), 0)

    def near_solve(f):
        def both(odd, half, sign):
            value = freq_ref[odd, 256 * half : 256 * half + 256]
            return jnp.where(left, value, sign * swap_halves(value))

        real, imag = both(0, 0, 1.0), both(0, 1, 1.0)
        odd_real, odd_imag = both(1, 0, -1.0), both(1, 1, -1.0)
        product = jnp.concatenate(
            [
                real * spectrum[0] - imag * spectrum[1],
                real * spectrum[1] + imag * spectrum[2],
                odd_real * spectrum[3] - odd_imag * spectrum[4],
                odd_real * spectrum[4] + odd_imag * spectrum[3],
            ],
            axis=0,
        )
        filtered = inverse_transform(idft_v, product).reshape(NB, 8, 128)
        first, onward = reduce_block(filtered, None, coefficient_load(0), odd_keep(FAR))
        ring = [(ring_ref[2 * i], ring_ref[2 * i + 1]) for i in range(4)]
        first = ring_solve(twin(first), twin(onward), ring, ring_ref[8], NEAR_STEPS, near_prev, near_ahead)
        solved = expand_block(first[0], near_ahead(first, 1)[0], NB, coefficient_load(0), odd_load(FAR))
        work[...] = solved.reshape(512, 128)

        for s in range(8):
            part = work[pl.ds(s, NB, stride=8), :]
            tiles = jnp.concatenate([part, pltpu.roll(part, 120, 1)], axis=0).T
            tiles = tiles.reshape(2, 4, 2, 8, 128)[:, :, 0]
            back_send[f, s] = tiles[0]
            back_send[f, 8 + s] = tiles[1]

        back_recv[f, me] = back_send[f, me]
        send_back(f)

    links_wait.wait_recv()
    kernel_rows()
    near_coefficients()
    each_slot(far_section)

    @functools.partial(each, NF)
    def _(f):
        near_rows(f)

        @functools.partial(each, 2)
        def _(odd):
            freq_ref[odd] = forward_transform(dft_v, odd, rows_ref[odd])

        pl.when(f == 0)(kernel_spectrum)
        near_solve(f)
        pl.when(f == 1)(lambda: each_slot(far_ring))

    for slot in range(2):
        sep_wait(slot, MEMBERS - 1).wait_recv()
    pl.when(member != 0)(lambda: sep_wait(2, 1).wait_recv())

    def far_expand(f, lt):
        w = f * FAR_TILES + lt
        lanes = pl.ds(pl.multiple_of(128 * lt + NEAR, 128), 128)
        solved = expand_block(sep_recv[w, 0], sep_recv[w, 1], NB, coefficient_load(lt + 1), odd_load(w))
        for j in range(NB):
            work[pl.ds(j, 8, stride=NB), :] = solved[j]
        out[f, :, lanes] = work[...]

    each(NF, lambda f: each(FAR_TILES, lambda lt: far_expand(f, lt)))

    kernel_wait.wait_send()
    links_wait.wait_send()
    near_wait(2).wait_send()
    for slot in range(2):
        far_wait(slot, MEMBERS - 1).wait_send()
    pl.when(member != 0)(lambda: far_wait(2, 1).wait_send())

    @each_slot
    def _(slot):
        slice_wait(slot, True).wait_send()
        sep_wait(slot, MEMBERS - 1).wait_send()

    @functools.partial(each, NF)
    def _(f):
        back_wait(f).wait_recv()

        for k in range(4):
            out[f, 128 * k : 128 * k + 128, 0:NEAR] = back_recv[f, :, k].reshape(128, 128).T

    each(NF, lambda f: back_wait(f).wait_send())


def body(fields, conduct, kernel):
    dft, idft = transforms()
    shape = fields.shape
    flat = fields.reshape(NF, NX * NB, shape[3])
    vmem = pltpu.VMEM
    dma = pltpu.SemaphoreType.DMA
    anywhere = pl.BlockSpec(memory_space=pl.ANY)
    inside = pl.BlockSpec(memory_space=pltpu.VMEM)
    ax_count = lax.axis_size("ax")
    out = pl.pallas_call(
        kernel_body,
        out_shape=vmem(flat.shape, F32),
        in_specs=[anywhere] * 5,
        out_specs=inside,
        scratch_shapes=[
            vmem((12, 512, 128), F32),
            vmem(conduct.shape, F32),
            vmem(kernel.shape, F32),
            vmem((2, 512, 512), F32),
            vmem((512, 1024), F32),
            vmem((4, 512, 512), BF16),
            vmem((2, 512, 1024), BF16),
            vmem((NF, NQ, 4, 8, 128), F32),
            vmem((NF, NQ, 4, 8, 128), F32),
            vmem((NF, NQ, 4, 8, 128), F32),
            vmem((NF, NQ, 4, 8, 128), F32),
            vmem((ax_count, 8, 128), F32),
            vmem((NQ, 8, 128), F32),
            vmem((NQ, 8, 128), F32),
            vmem((512, 128), F32),
            vmem((2, 128, 512), F32),
            vmem((2, 512, 128), F32),
            vmem((5, 256, 128), F32),
            vmem((4 + SLOTS, NB, 8, 128), F32),
            vmem((4 + SLOTS, NB, 8, 128), F32),
            vmem((4 + SLOTS, NB, 8, 128), F32),
            vmem((9, 2, 8, 128), F32),
            vmem((FAR + 1 + SLOTS, NB, 8, 128), F32),
            vmem((512, 128), F32),
            vmem((FAR, 3, 8, 128), F32),
            vmem((SLOTS, MEMBERS, 3, 8, 128), F32),
            vmem((SLOTS, 3, 8, 128), F32),
            vmem((SLOTS, SLICES, 3, 8, 128), F32),
            vmem((SLOTS, 2, SLICES, 8, 128), F32),
            vmem((SLOTS, MEMBERS, 2, 8, 128), F32),
            vmem((FAR, 2, 8, 128), F32),
            dma((12,)), dma((4,)),
            dma((NF,)), dma((NF,)), dma((NF,)), dma((NF,)),
            dma, dma, dma, dma,
            dma((SLOTS,)), dma((SLOTS,)), dma((SLOTS,)), dma((SLOTS,)), dma((SLOTS,)), dma((SLOTS,)),
        ],
        compiler_params=pltpu.CompilerParams(
            collective_id=0, has_side_effects=True, vmem_limit_bytes=int(60.9 * 2**20)
        ),
    )(flat, conduct, kernel, jnp.asarray(dft), jnp.asarray(idft))
    return out.reshape(shape)


def solution(mesh):
    return jax.shard_map(
        body,
        mesh=mesh,
        in_specs=(P(None, "ax", "az", None), P("az", None), P("ax", "az")),
        out_specs=P(None, "ax", "az", None),
        check_vma=False,
    )
```

```python
import functools

import jax
import jax.numpy as jnp
import numpy as np
from jax import lax
from jax.experimental import pallas as pl
from jax.experimental.pallas import tpu as pltpu
from jax.sharding import PartitionSpec as P

MESH = pl.DeviceIdType.MESH
F32 = jnp.float32
BF16 = jnp.bfloat16

NF = 3
NX = 8
NB = 64
NQ = 16
HALF = NB * NQ // 2
NEAR = 128
FAR_TILES = 3
FAR = NF * FAR_TILES
MEMBERS = 4
SLICES = NQ // MEMBERS
SLOTS = 3
NEAR_STEPS = (1, 2, 4, 8)
FAR_STEPS = (1, 2)
ORDER = (8, 4, 12, 1, 9, 5, 13, 2, 10, 6, 14, 3, 11, 7, 15)


def transforms():
    points = 2 * HALF
    j = np.arange(HALF)
    forward, inverse = [], []
    for odd in (0, 1):
        freq = 2 * np.arange(HALF // 2) + odd
        angle = 2.0 * np.pi * ((freq[:, None] * j[None, :]) % points) / points
        real, imag = np.cos(angle), -np.sin(angle)
        scale = np.full((HALF // 2, 1), 2.0 / points)
        real_back, imag_back = real * scale, imag * scale
        if not odd:
            imag[0] = np.cos(np.pi * j)
            real_back[0] = 1.0 / points
            imag_back[0] = imag[0] / points
        forward.append(np.concatenate([real, imag]))
        inverse.append(np.concatenate([real_back, imag_back]))
    order = (NB * np.arange(8)[None, :] + np.arange(NB)[:, None]).reshape(-1)
    back = np.concatenate(inverse, axis=0).T[order]
    return np.stack(forward).astype(np.float32), back.astype(np.float32)


def split(x):
    high = x.astype(BF16)
    return high, (x - high.astype(F32)).astype(BF16)


def forward_transform(dft_ref, which, rows):
    high, low = split(rows)
    both = jnp.concatenate([high, low], axis=0)
    contract = (((1,), (1,)), ((), ()))
    one = lax.dot_general(dft_ref[2 * which], both, contract, preferred_element_type=F32)
    two = lax.dot_general(dft_ref[2 * which + 1], high, contract, preferred_element_type=F32)
    return one[:, :128] + one[:, 128:] + two


def inverse_transform(idft_ref, spectrum):
    high, low = split(spectrum)
    both = jnp.concatenate([high, low], axis=1)
    contract = (((1,), (0,)), ((), ()))
    one = lax.dot_general(idft_ref[0], both, contract, preferred_element_type=F32)
    two = lax.dot_general(idft_ref[1], high, contract, preferred_element_type=F32)
    return one[:, :128] + one[:, 128:] + two


def place(count):
    return NB - 2 * count


def coefficients(links, excess, onward, store):
    while links.shape[0] > 1:
        count = links.shape[0] // 2
        pairs = links.reshape(count, 2, 8, 128)
        behind, ahead = pairs[:, 0], pairs[:, 1]
        own = excess.reshape(count, 2, 8, 128)
        inv = 1.0 / (behind + ahead + own[:, 1])
        alpha, beta = behind * inv, ahead * inv
        store(place(count), alpha, beta, inv)
        to_left, to_right = alpha * own[:, 1], beta * own[:, 1]
        excess = own[:, 0] + to_left
        if count > 1:
            excess = jnp.concatenate([excess[:1], excess[1:] + to_right[:-1]], axis=0)
        onward = to_right[count - 1] if onward is None else onward + to_right[count - 1]
        links = behind * beta
    return links[0], excess[0], onward


def reduce_block(values, onward, load, keep):
    while values.shape[0] > 1:
        count = values.shape[0] // 2
        pairs = values.reshape(count, 2, 8, 128)
        even, odd = pairs[:, 0], pairs[:, 1]
        keep(place(count), odd)
        alpha, beta, _ = load(place(count), count)
        to_right = beta * odd
        values = even + alpha * odd
        if count > 1:
            values = jnp.concatenate([values[:1], values[1:] + to_right[:-1]], axis=0)
        onward = to_right[count - 1] if onward is None else onward + to_right[count - 1]
    return values[0], onward


def expand_block(first, following, length, load, kept):
    solved = first[None]
    while solved.shape[0] < length:
        count = solved.shape[0]
        alpha, beta, inv = load(place(count), count)
        right = following[None]
        if count > 1:
            right = jnp.concatenate([solved[1:], right], axis=0)
        odd = inv * kept(place(count), count) + alpha * solved + beta * right
        solved = jnp.stack([solved, odd], axis=1).reshape(2 * count, 8, 128)
    return solved


def ring_coefficients(link, first, onward, steps, prev, ahead):
    excess = first + prev(onward, 1)
    after, before = link, prev(link, 1)
    levels = []
    for d in steps:
        inv = 1.0 / (excess + before + after)
        alpha, beta = before * prev(inv, d), after * ahead(inv, d)
        levels.append((alpha, beta))
        excess = excess + alpha * prev(excess, d) + beta * ahead(excess, d)
        if d < steps[-1]:
            before, after = alpha * prev(before, d), beta * ahead(after, d)
    return levels, 1.0 / excess


def ring_solve(first, onward, levels, final, steps, prev, ahead):
    value = first + prev(onward, 1)
    for d, (alpha, beta) in zip(steps, levels):
        value = value + alpha * prev(value, d) + beta * ahead(value, d)
    return value * final


def far_prev(v, d):
    return jnp.concatenate([v[-d:], v[:-d]], axis=0)


def far_ahead(v, d):
    return jnp.concatenate([v[d:], v[:d]], axis=0)


def twin(v):
    return jnp.stack([v, pltpu.roll(v, 64, 1)])


def near_shift(v, d, ahead):
    if d == 8:
        return jnp.stack([v[1], v[0]])
    row = lax.broadcasted_iota(jnp.int32, (8, 128), 0)
    inside = row < 8 - d if ahead else row >= d
    turn = 8 - d if ahead else d
    one, two = pltpu.roll(v[0], turn, 0), pltpu.roll(v[1], turn, 0)
    return jnp.stack([jnp.where(inside, one, two), jnp.where(inside, two, one)])


def near_prev(v, d):
    return near_shift(v, d, False)


def near_ahead(v, d):
    return near_shift(v, d, True)


def swap_halves(x):
    return pltpu.roll(x, 64, x.ndim - 1)


def each(count, step):
    def run(i, carry):
        step(i)
        return carry

    lax.fori_loop(0, count, run, 0)


def wrap(i, count):
    return jnp.where(i >= count, i - count, i)


def kernel_body(
    fields, conduct_hbm, kernel_hbm, dft, idft, out,
    held, conduct, kernel, dft_raw, idft_raw, dft_v, idft_v, near_send, near_recv, back_send, back_recv,
    kernel_all, links_send, links_recv, link_rows, rows_ref, freq_ref, spectrum,
    alpha_ref, beta_ref, inv_ref, ring_ref, odd_ref, work,
    far_send, far_recv, slice_send, slice_recv, ring_values, sep_send, sep_recv,
    load_sem, const_sem, ns, nr, bs, br, ks, kr, cs, cr, fs, fr, xs, xr, ss, sr,
):
    me = lax.axis_index("az")
    mx = lax.axis_index("ax")
    ax_count = lax.axis_size("ax")
    member, section = lax.rem(me, MEMBERS), me // MEMBERS
    others = NQ - 1

    def peer(k):
        return wrap(me + k, NQ)

    def plane(k):
        return wrap(mx + k, ax_count)

    def mate(k):
        return wrap(member + k, MEMBERS)

    def remote(src, dst, send, recv, az, ax):
        return pltpu.make_async_remote_copy(
            src, dst, send, recv, device_id={"az": az, "ax": ax}, device_id_type=MESH
        )

    barrier = pltpu.get_barrier_semaphore()

    for k in ORDER:
        pl.semaphore_signal(barrier, inc=1, device_id={"az": peer(k), "ax": mx}, device_id_type=MESH)
    for k in range(1, ax_count):
        pl.semaphore_signal(barrier, inc=1, device_id={"az": me, "ax": plane(k)}, device_id_type=MESH)

    def load(f, tile):
        return pltpu.make_async_copy(
            fields.at[f, :, pl.ds(pl.multiple_of(128 * tile, 128), 128)], held.at[f * 4 + tile], load_sem.at[f * 4 + tile]
        )

    small_loads = [
        pltpu.make_async_copy(kernel_hbm, kernel, const_sem.at[2]),
        pltpu.make_async_copy(conduct_hbm, conduct, const_sem.at[3]),
    ]
    const_loads = [
        pltpu.make_async_copy(dft, dft_raw, const_sem.at[0]),
        pltpu.make_async_copy(idft, idft_raw, const_sem.at[1]),
    ]
    each(NF, lambda f: load(f, 0).start())
    for copy in small_loads:
        copy.start()
    each(NF, lambda f: each(FAR_TILES, lambda lt: load(f, lt + 1).start()))
    for copy in const_loads:
        copy.start()

    def transpose_near(f):
        load(f, 0).wait()

        for k in range(4):
            near_send[f, :, k] = held[f * 4, 128 * k : 128 * k + 128, :].T.reshape(NQ, 8, 128)

        near_recv[f, me] = near_send[f, me]

    transpose_near(0)
    for copy in small_loads:
        copy.wait()
    kernel_all[mx] = jnp.concatenate([kernel[0:8, :], kernel[8:16, :]], axis=1)

    pl.semaphore_wait(barrier, others + ax_count - 1)


    kernel_whole = kernel_all.at[pl.ds(0, ax_count - 1)]
    kernel_wait = remote(kernel_whole, kernel_whole, ks, kr, me, plane(1))

    def send_near(f):
        for k in map(peer, ORDER):
            remote(near_send.at[f, k], near_recv.at[f, me], ns.at[f], nr.at[f], k, mx).start()

    def near_wait(f):
        whole = pl.ds(0, others)
        return remote(near_send.at[f, whole], near_recv.at[f, whole], ns.at[f], nr.at[f], peer(1), mx)

    send_near(0)
    for k in range(1, ax_count):
        remote(kernel_all.at[mx], kernel_all.at[mx], ks, kr, me, plane(k)).start()
    transpose_near(1)
    transpose_near(2)
    row = lax.broadcasted_iota(jnp.int32, (8, 128), 0)
    lane = lax.broadcasted_iota(jnp.int32, (8, 128), 1)

    def coefficient_store(c):
        def store(offset, alpha, beta, inv):
            count = alpha.shape[0]
            alpha_ref[c, offset : offset + count] = alpha
            beta_ref[c, offset : offset + count] = beta
            inv_ref[c, offset : offset + count] = inv

        return store

    def coefficient_load(c):
        def load(offset, count):
            return (
                alpha_ref[c, offset : offset + count],
                beta_ref[c, offset : offset + count],
                inv_ref[c, offset : offset + count],
            )

        return load

    def odd_keep(w):
        def keep(offset, value):
            odd_ref[w, offset : offset + value.shape[0]] = value

        return keep

    def odd_load(w):
        return lambda offset, count: odd_ref[w, offset : offset + count]

    unit = jnp.ones((NB, 8, 128), F32)

    def packed(link, first, onward):
        return jnp.where(row == 0, link, jnp.where(row == 1, first, onward))

    @functools.partial(each, FAR_TILES)
    def _(lt):
        lanes = pl.ds(pl.multiple_of(128 * lt + NEAR, 128), 128)
        links = jnp.stack([jnp.broadcast_to(conduct[j : j + 1, lanes], (8, 128)) for j in range(NB)])
        tile = packed(*coefficients(links, unit, None, coefficient_store(lt + 1)))
        for f in range(NF):
            far_send[f * FAR_TILES + lt, 2] = tile

    each(NF, lambda f: each(FAR_TILES, lambda lt: load(f, lt + 1).wait()))

    def far_reduce(f, lt):
        w = f * FAR_TILES + lt
        values = jnp.stack([held[f * 4 + lt + 1, pl.ds(j, 8, stride=NB), :] for j in range(NB)])
        first, onward = reduce_block(values, None, coefficient_load(lt + 1), odd_keep(w))
        far_send[w, 0] = first
        far_send[w, 1] = onward

    each(NF, lambda f: each(FAR_TILES, lambda lt: far_reduce(f, lt)))

    for w in range(FAR):
        slot, owner = w // MEMBERS, w % MEMBERS

        @pl.when(member == owner)
        def _():
            far_recv[slot, member] = far_send[w]

        @pl.when(member != owner)
        def _():
            remote(
                far_send.at[w], far_recv.at[slot, member], fs.at[slot], fr.at[slot], MEMBERS * section + owner, mx
            ).start()

    def far_wait(slot, count):
        return remote(
            far_send.at[pl.ds(0, count)], far_recv.at[slot, pl.ds(0, count)], fs.at[slot], fr.at[slot],
            MEMBERS * section + mate(1), mx,
        )

    near_links = conduct[:, :NEAR]
    near_links = jnp.concatenate([near_links, near_links], axis=0).T.reshape(NQ, 8, 128)
    kernel_wait.wait_recv()
    kernels = kernel_all[...]
    swapped = swap_halves(kernels.reshape(64, 128)).reshape(8, 8, 128)
    kernels = jnp.stack([swapped, kernels], axis=1).reshape(NQ, 8, 128)
    links_send[...] = jnp.where(lane[None] < 64, near_links, kernels)
    links_recv[me] = links_send[me]

    for k in map(peer, ORDER):
        remote(links_send.at[k], links_recv.at[me], cs, cr, k, mx).start()

    links_wait = remote(links_send.at[pl.ds(0, others)], links_recv.at[pl.ds(0, others)], cs, cr, peer(1), mx)
    near_wait(0).wait_send()
    send_near(1)

    for copy in const_loads:
        copy.wait()
    for odd in range(2):
        dft_v[2 * odd], dft_v[2 * odd + 1] = split(dft_raw[odd])
    idft_v[0], idft_v[1] = split(idft_raw[...])

    near_wait(1).wait_send()
    send_near(2)

    def far_section(slot):
        far_wait(slot, MEMBERS - 1).wait_recv()
        shape = (MEMBERS, 8, 128)
        link, first, onward = [jnp.broadcast_to(far_recv[slot, :, 2, i : i + 1, :], shape) for i in range(3)]
        first = jnp.concatenate([first[:1], first[1:] + onward[:-1]], axis=0)
        tile = packed(*coefficients(link, first, onward[MEMBERS - 1], coefficient_store(4 + slot)))
        values, onward = far_recv[slot, :, 0], far_recv[slot, :, 1]
        values = jnp.concatenate([values[:1], values[1:] + onward[:-1]], axis=0)
        value, onward = reduce_block(values, onward[MEMBERS - 1], coefficient_load(4 + slot), odd_keep(FAR + 1 + slot))
        slice_send[slot, 0] = value
        slice_send[slot, 1] = onward
        slice_send[slot, 2] = tile
        slice_recv[slot, section] = slice_send[slot]
        for k in range(1, SLICES):
            remote(
                slice_send.at[slot], slice_recv.at[slot, section], xs.at[slot], xr.at[slot], peer(MEMBERS * k), mx
            ).start()

    def slice_wait(slot, sending):
        part = pl.ds(0, SLICES - 1)
        return remote(slice_recv.at[slot, part], slice_recv.at[slot, part], xs.at[slot], xr.at[slot], peer(MEMBERS), mx)

    def far_ring(slot):
        slice_wait(slot, False).wait_recv()
        spread = [jnp.broadcast_to(slice_recv[slot, :, 2, i : i + 1, :], (SLICES, 8, 128)) for i in range(3)]
        levels, final = ring_coefficients(*spread, FAR_STEPS, far_prev, far_ahead)
        value = ring_solve(slice_recv[slot, :, 0], slice_recv[slot, :, 1], levels, final, FAR_STEPS, far_prev, far_ahead)
        ring_values[slot, 0] = value
        ring_values[slot, 1] = far_ahead(value, 1)
        following = ring_values[slot, 1, section]
        solved = expand_block(
            ring_values[slot, 0, section], following, MEMBERS, coefficient_load(4 + slot), odd_load(FAR + 1 + slot)
        )
        sep_send[slot, :, 0] = solved
        sep_send[slot, :, 1] = jnp.concatenate([solved[1:], following[None]], axis=0)
        sep_recv[MEMBERS * slot + member] = sep_send[slot, member]
        for k in range(1, MEMBERS):
            remote(
                sep_send.at[slot, mate(k)], sep_recv.at[MEMBERS * slot + member], ss.at[slot], sr.at[slot],
                MEMBERS * section + mate(k), mx,
            ).start()

    def sep_wait(slot, count):
        return remote(
            sep_send.at[slot, pl.ds(0, count)], sep_recv.at[pl.ds(0, count)], ss.at[slot], sr.at[slot],
            MEMBERS * section + mate(1), mx,
        )

    def each_slot(step):
        @functools.partial(each, SLOTS)
        def _(slot):
            pl.when(MEMBERS * slot + member < FAR)(lambda: step(slot))

    def send_back(f):
        for k in map(peer, ORDER):
            remote(back_send.at[f, k], back_recv.at[f, me], bs.at[f], br.at[f], k, mx).start()

    def back_wait(f):
        whole = pl.ds(0, others)
        return remote(back_send.at[f, whole], back_recv.at[f, whole], bs.at[f], br.at[f], peer(1), mx)

    def lay_rows(points, place):
        total, difference = points[:4] + points[4:], points[:4] - points[4:]
        rows_ref[0, place : place + 64] = jnp.concatenate([total[m] for m in range(4)], axis=1)
        rows_ref[1, place : place + 64] = jnp.concatenate([difference[m] for m in range(4)], axis=1)

    def kernel_rows():
        pieces = links_recv[...].reshape(8, 2, 8, 128)
        lags = jnp.where(lane[None] < 64, swap_halves(pieces[:, 0].reshape(64, 128)).reshape(8, 8, 128), pieces[:, 1])
        lay_rows(jnp.concatenate([lags] * 8, axis=1), 64)

    left = lax.broadcasted_iota(jnp.int32, (256, 128), 1) < 64

    def kernel_spectrum():
        def both(odd, half):
            value = freq_ref[odd, 256 * half : 256 * half + 256]
            return jnp.where(left, swap_halves(value), value)

        first_row = lax.broadcasted_iota(jnp.int32, (256, 128), 0) == 0
        real, imag = both(0, 0), both(0, 1)
        spectrum[0] = real
        spectrum[1] = jnp.where(first_row, 0.0, imag)
        spectrum[2] = jnp.where(first_row, imag, real)
        spectrum[3] = both(1, 0)
        spectrum[4] = both(1, 1)

    def near_coefficients():
        for s in range(8):
            rows = jnp.concatenate([links_recv[s]] * 8 + [links_recv[8 + s]] * 8, axis=0)
            link_rows[pl.ds(s, NB, stride=8), :] = rows.T[:NB]

        reduced = coefficients(link_rows[...].reshape(NB, 8, 128), unit, None, coefficient_store(0))
        levels, final = ring_coefficients(*[twin(v) for v in reduced], NEAR_STEPS, near_prev, near_ahead)
        for index, (alpha, beta) in enumerate(levels):
            ring_ref[2 * index] = alpha
            ring_ref[2 * index + 1] = beta
        ring_ref[8] = final

    def near_rows(f):
        near_wait(f).wait_recv()
        pieces = near_recv[f].reshape(8, 2, 4, 8, 128)
        low, high = pieces[:, 0].reshape(256, 128), pieces[:, 1].reshape(256, 128)
        plane_a = jnp.where(left, low, swap_halves(high)).reshape(8, 4, 8, 128)
        plane_b = jnp.where(left, swap_halves(low), high).reshape(8, 4, 8, 128)
        lay_rows(jnp.stack([plane_a, plane_b], axis=2).reshape(8, 64, 128), 0)

    def near_solve(f):
        def both(odd, half, sign):
            value = freq_ref[odd, 256 * half : 256 * half + 256]
            return jnp.where(left, value, sign * swap_halves(value))

        real, imag = both(0, 0, 1.0), both(0, 1, 1.0)
        odd_real, odd_imag = both(1, 0, -1.0), both(1, 1, -1.0)
        product = jnp.concatenate(
            [
                real * spectrum[0] - imag * spectrum[1],
                real * spectrum[1] + imag * spectrum[2],
                odd_real * spectrum[3] - odd_imag * spectrum[4],
                odd_real * spectrum[4] + odd_imag * spectrum[3],
            ],
            axis=0,
        )
        filtered = inverse_transform(idft_v, product).reshape(NB, 8, 128)
        first, onward = reduce_block(filtered, None, coefficient_load(0), odd_keep(FAR))
        ring = [(ring_ref[2 * i], ring_ref[2 * i + 1]) for i in range(4)]
        first = ring_solve(twin(first), twin(onward), ring, ring_ref[8], NEAR_STEPS, near_prev, near_ahead)
        solved = expand_block(first[0], near_ahead(first, 1)[0], NB, coefficient_load(0), odd_load(FAR))
        work[...] = solved.reshape(512, 128)

        for s in range(8):
            part = work[pl.ds(s, NB, stride=8), :]
            tiles = jnp.concatenate([part, pltpu.roll(part, 120, 1)], axis=0).T
            tiles = tiles.reshape(2, 4, 2, 8, 128)[:, :, 0]
            back_send[f, s] = tiles[0]
            back_send[f, 8 + s] = tiles[1]

        back_recv[f, me] = back_send[f, me]
        send_back(f)

    links_wait.wait_recv()
    kernel_rows()
    near_coefficients()
    each_slot(far_section)

    @functools.partial(each, NF)
    def _(f):
        near_rows(f)

        @functools.partial(each, 2)
        def _(odd):
            freq_ref[odd] = forward_transform(dft_v, odd, rows_ref[odd])

        pl.when(f == 0)(kernel_spectrum)
        near_solve(f)
        pl.when(f == 1)(lambda: each_slot(far_ring))

    for slot in range(2):
        sep_wait(slot, MEMBERS - 1).wait_recv()
    pl.when(member != 0)(lambda: sep_wait(2, 1).wait_recv())

    def far_expand(f, lt):
        w = f * FAR_TILES + lt
        lanes = pl.ds(pl.multiple_of(128 * lt + NEAR, 128), 128)
        solved = expand_block(sep_recv[w, 0], sep_recv[w, 1], NB, coefficient_load(lt + 1), odd_load(w))
        for j in range(NB):
            work[pl.ds(j, 8, stride=NB), :] = solved[j]
        out[f, :, lanes] = work[...]

    each(NF, lambda f: each(FAR_TILES, lambda lt: far_expand(f, lt)))

    kernel_wait.wait_send()
    links_wait.wait_send()
    near_wait(2).wait_send()
    for slot in range(2):
        far_wait(slot, MEMBERS - 1).wait_send()
    pl.when(member != 0)(lambda: far_wait(2, 1).wait_send())

    @each_slot
    def _(slot):
        slice_wait(slot, True).wait_send()
        sep_wait(slot, MEMBERS - 1).wait_send()

    @functools.partial(each, NF)
    def _(f):
        back_wait(f).wait_recv()

        for k in range(4):
            out[f, 128 * k : 128 * k + 128, 0:NEAR] = back_recv[f, :, k].reshape(128, 128).T

    each(NF, lambda f: back_wait(f).wait_send())


def body(fields, conduct, kernel):
    dft, idft = transforms()
    shape = fields.shape
    flat = fields.reshape(NF, NX * NB, shape[3])
    vmem = pltpu.VMEM
    dma = pltpu.SemaphoreType.DMA
    anywhere = pl.BlockSpec(memory_space=pl.ANY)
    inside = pl.BlockSpec(memory_space=pltpu.VMEM)
    ax_count = lax.axis_size("ax")
    out = pl.pallas_call(
        kernel_body,
        out_shape=vmem(flat.shape, F32),
        in_specs=[anywhere] * 5,
        out_specs=inside,
        scratch_shapes=[
            vmem((12, 512, 128), F32),
            vmem(conduct.shape, F32),
            vmem(kernel.shape, F32),
            vmem((2, 512, 512), F32),
            vmem((512, 1024), F32),
            vmem((4, 512, 512), BF16),
            vmem((2, 512, 1024), BF16),
            vmem((NF, NQ, 4, 8, 128), F32),
            vmem((NF, NQ, 4, 8, 128), F32),
            vmem((NF, NQ, 4, 8, 128), F32),
            vmem((NF, NQ, 4, 8, 128), F32),
            vmem((ax_count, 8, 128), F32),
            vmem((NQ, 8, 128), F32),
            vmem((NQ, 8, 128), F32),
            vmem((512, 128), F32),
            vmem((2, 128, 512), F32),
            vmem((2, 512, 128), F32),
            vmem((5, 256, 128), F32),
            vmem((4 + SLOTS, NB, 8, 128), F32),
            vmem((4 + SLOTS, NB, 8, 128), F32),
            vmem((4 + SLOTS, NB, 8, 128), F32),
            vmem((9, 2, 8, 128), F32),
            vmem((FAR + 1 + SLOTS, NB, 8, 128), F32),
            vmem((512, 128), F32),
            vmem((FAR, 3, 8, 128), F32),
            vmem((SLOTS, MEMBERS, 3, 8, 128), F32),
            vmem((SLOTS, 3, 8, 128), F32),
            vmem((SLOTS, SLICES, 3, 8, 128), F32),
            vmem((SLOTS, 2, SLICES, 8, 128), F32),
            vmem((SLOTS, MEMBERS, 2, 8, 128), F32),
            vmem((FAR, 2, 8, 128), F32),
            dma((12,)), dma((4,)),
            dma((NF,)), dma((NF,)), dma((NF,)), dma((NF,)),
            dma, dma, dma, dma,
            dma((SLOTS,)), dma((SLOTS,)), dma((SLOTS,)), dma((SLOTS,)), dma((SLOTS,)), dma((SLOTS,)),
        ],
        compiler_params=pltpu.CompilerParams(
            collective_id=0, has_side_effects=True, vmem_limit_bytes=int(60.9 * 2**20)
        ),
    )(flat, conduct, kernel, jnp.asarray(dft), jnp.asarray(idft))
    return out.reshape(shape)


def solution(mesh):
    return jax.shard_map(
        body,
        mesh=mesh,
        in_specs=(P(None, "ax", "az", None), P("az", None), P("ax", "az")),
        out_specs=P(None, "ax", "az", None),
        check_vma=False,
    )
```
